256 devices in a mesh: half: 2 (over core), cls: 32 (over y, z), tile: 4 (over x).
Axes of the slice: x: 4, y: 4, z: 8, core: 2. Of those that a mesh axis runs over, the one named last changes fastest.
Arguments:
- images: bfloat16 [8192, 256, 256], P(('half', 'cls', 'tile')), may hold values from -32 to 32
- references: bfloat16 [2, 64, 256, 256], P('half', 'cls'), may hold values from -16 to 16
- image_owner: int32 [8192, 1], P(('half', 'cls', 'tile')), may hold values from 0 to 31; in each aligned block of 32 rows (0 to 31, 32 to 63, ...) at most 2 rows name the same one
- image_class: int32 [8192], P(('half', 'cls', 'tile')), may hold values from 0 to 1
- defocus_bin: int32 [8192], P(('half', 'cls', 'tile')), may hold values from 0 to 15
- slice_cells: int32 [64, 128], replicated, may hold values from 0 to 16383, as said below
Outputs:
- half_maps: float32 [2, 16384, 256], P('half', ('cls', 'tile'))
The draws below stay inside these ranges and needn't reach their ends.
Inputs may be any that keep to these rules, and one draw needn't show every extreme that they name: `image_owner`: among the 32 images of one device no owner is named more than 2 times, and in every draw some device names some owner exactly 2 times. `slice_cells`: take the 256 entries of the classes of one owner (rows o * 2 to o * 2 + 1) and the blocks of 128 consecutive cells: no block holds more than 4 of these entries, and for every owner some block holds exactly 4.
All inputs are finite; a program needn't handle non-finite values.
Results may differ from the reference program's by a relative error of at most 0.008.
Values may be sent and summed in bfloat16 or wider, within the bound.
A program may use at most 128 MiB of HBM per device.

```python
import math
import jax
import jax.numpy as jnp
import numpy as np
from jax import lax

PIX = 256
KF = 128
IMG_DEV = 32
CLS_DEV = 2
BINS = 16
CAP = 2
CLASSES = 64
IMAGES = 8192
CELLS = 16384
SHELLS = 64
NBLOCK = 128
CELLS_DEV = 128
ROW_CAP = 4
N_CLS = 32


def shared_template(key):
    return jax.random.normal(key, (PIX, PIX), jnp.float32)


def draw_images(key, part):
    template = shared_template(key)
    key = jax.random.fold_in(key, 11)
    shift_key, noise_key, scale_key = jax.random.split(key, 3)
    offsets = jax.random.randint(shift_key, (IMAGES, 2), 0, PIX)
    noise_field = jax.random.normal(noise_key, (IMAGES, PIX, PIX), jnp.float32)
    spread = jnp.exp(jax.random.uniform(scale_key, (IMAGES, 1, 1), jnp.float32, math.log(0.5), math.log(2.0)))
    shifted = jax.vmap(lambda offset_pair: jnp.roll(template, (offset_pair[0], offset_pair[1]), axis=(0, 1)))(offsets)
    return jnp.clip(shifted + spread * noise_field, -32.0, 32.0).astype(jnp.bfloat16)


def draw_references(key, part):
    template = shared_template(key)
    key = jax.random.fold_in(key, 23)
    noise_field = 0.5 * jax.random.normal(key, (2, CLASSES, PIX, PIX), jnp.float32)
    return jnp.clip(template[None, None, :, :] + noise_field, -16.0, 16.0).astype(jnp.bfloat16)


def owner_cells(owner_key):
    order_key, special_key, shuffle_key, cell_key = jax.random.split(owner_key, 4)
    total_slots = NBLOCK * ROW_CAP
    row_total = CLS_DEV * KF
    order = jax.random.permutation(order_key, total_slots)
    rank = jnp.argsort(order).astype(jnp.int32)
    special = jax.random.randint(special_key, (), 0, NBLOCK)
    slot_ids = jnp.arange(total_slots, dtype=jnp.int32)
    score = jnp.where(slot_ids // ROW_CAP == special, rank - total_slots, rank)
    chosen = jnp.argsort(score).astype(jnp.int32)[:row_total]
    blocks = (chosen // ROW_CAP)[jax.random.permutation(shuffle_key, row_total)]
    inner = jax.random.randint(cell_key, (row_total,), 0, CELLS_DEV)
    return (blocks * CELLS_DEV + inner).astype(jnp.int32)


def draw_slice_cells(key, part):
    key = jax.random.fold_in(key, 37)
    owner_keys = jax.random.split(key, N_CLS)
    return jax.vmap(owner_cells)(owner_keys).reshape(CLASSES, KF)


def plant(result, stream_key, smallest, high):
    spot = [jax.random.randint(jax.random.fold_in(stream_key, axis), (), 0, length) for axis, length in enumerate(result.shape)]
    longest = result.shape.index(max(result.shape))
    neighbour = spot[:longest] + [(spot[longest] + 1) % result.shape[longest]] + spot[longest + 1:]
    return result.at[tuple(spot)].set(smallest).at[tuple(neighbour)].set(high)


def deal_out(own_key, own, number, rows, amount, top, bound, skew):
    order = jax.random.permutation(own_key, amount)
    heavy_load, common = load_shares(amount, rows * top, bound, skew, True), load_shares(amount, rows * top, bound, skew, False)
    places = jnp.arange(amount)

    def named(sizes, rotation):
        used = int((sizes > 0).sum())
        fixed = max(1, used // 4)
        moved = fixed + (places - fixed + rotation * (used - fixed)) % max(1, amount - fixed)
        return jnp.zeros((amount,), jnp.int32).at[order[jnp.where(places < fixed, places, moved)]].set(jnp.asarray(sizes, jnp.int32))

    sizes = jnp.where(number % 4 == 0, named(heavy_load, number // 4), named(common, number - number // 4 - 1))
    mixed = jax.random.permutation(jax.random.fold_in(own, 3), amount)
    giver, sink = mixed[0:amount // 2 * 2:2], mixed[1:amount // 2 * 2:2]
    slack = jnp.minimum(sizes[giver] - 1, bound - sizes[sink]) // 2
    slack = jnp.where((giver == order[0]) | (sink == order[0]) | (sizes[sink] == 0), 0, jnp.maximum(slack, 0))
    moved = jax.random.randint(jax.random.fold_in(own, 4), (amount // 2,), 0, 1 << 20) % (slack + 1)
    sizes = sizes.at[giver].add(-moved).at[sink].add(moved)
    items = jnp.searchsorted(jnp.cumsum(sizes), jnp.arange(rows * top), side="right").astype(jnp.int32)
    grid = items.reshape(top, rows).T
    grid = grid[jax.random.permutation(jax.random.fold_in(own, 1), rows)]
    rotation = jax.random.randint(jax.random.fold_in(own, 2), (rows, 1), 0, top)
    return jnp.take_along_axis(grid, (jnp.arange(top)[None, :] + rotation) % top, axis=1)


def load_shares(amount, total, reach, slope, full):
    portions = [(1 << 20) // math.isqrt(rank ** slope) + 1 for rank in range(1, amount + 1)]
    largest = reach if full else min(reach, max(-(-total // amount), total * portions[0] // sum(portions)))
    least = 1 if total - largest >= amount - 1 else 0
    counts, surplus = [largest] + [least] * (amount - 1), total - largest - least * (amount - 1)
    while surplus > 0:
        candidates = [i for i in range(1, amount) if counts[i] < largest] or [i for i in range(1, amount) if counts[i] < reach]
        pool, left = sum([portions[i] for i in candidates]), surplus
        for i in candidates:
            more = min(reach - counts[i], max(1, left * portions[i] // pool), surplus)
            counts[i] = counts[i] + more
            surplus = surplus - more
    return np.array(counts)


def setup_inputs(seed: int = 0) -> dict:
    key_of = jax.random.split(jax.random.key(seed), 7)
    images = draw_images(jax.random.fold_in(key_of[6], 71), 0)
    references = draw_references(jax.random.fold_in(key_of[6], 71), 0)
    image_owner_keys = jax.random.split(jax.random.fold_in(key_of[2], 1), IMAGES // IMG_DEV)
    image_owner_turns = jax.random.permutation(jax.random.fold_in(key_of[2], 3), IMAGES // IMG_DEV)
    image_owner = jax.vmap(lambda own, number: deal_out(jax.random.fold_in(key_of[2], 2), own, number, IMG_DEV, N_CLS, 1, CAP, 2))(image_owner_keys, image_owner_turns).reshape((IMAGES, 1))
    image_class = plant(jax.random.randint(key_of[3], (IMAGES,), 0, CLS_DEV), jax.random.fold_in(key_of[3], 1), 0, CLS_DEV - 1).astype(jnp.int32)
    defocus_bin = plant(jax.random.randint(key_of[4], (IMAGES,), 0, BINS), jax.random.fold_in(key_of[4], 1), 0, BINS - 1).astype(jnp.int32)
    slice_cells = draw_slice_cells(jax.random.fold_in(key_of[6], 71), 0)
    return {"images": images, "references": references, "image_owner": image_owner, "image_class": image_class, "defocus_bin": defocus_bin, "slice_cells": slice_cells}


sharpness = 40.0
ctf_scale = 6.0
amp_phase = 0.1

def dft_tables():
    sample_pos = jnp.arange(PIX, dtype=jnp.int32)[:, None]
    freq_pos = jnp.arange(KF, dtype=jnp.int32)[None, :] - KF // 2
    angles = (sample_pos * freq_pos % PIX).astype(jnp.float32) * (2.0 * math.pi / PIX)
    scaling = 1.0 / math.sqrt(PIX)
    return ((jnp.cos(angles) * scaling).astype(jnp.bfloat16), (jnp.sin(angles) * scaling).astype(jnp.bfloat16))

def forward(planes, cos_table, sin_table):
    number = planes.shape[0]
    section_one = jnp.dot(planes.reshape(number * PIX, PIX), jnp.concatenate([cos_table, sin_table], 1), preferred_element_type=jnp.float32)
    section_one = section_one.astype(jnp.bfloat16).reshape(number, PIX, 2 * KF)
    stacked = jnp.concatenate([cos_table.T, sin_table.T], 0)
    section_two = jnp.einsum('kp,npq->nkq', stacked.astype(jnp.float32), section_one.astype(jnp.float32))
    cos_p = section_two[:, :KF, :KF]
    cos_q = section_two[:, :KF, KF:]
    sin_p = section_two[:, KF:, :KF]
    sin_q = section_two[:, KF:, KF:]
    return jnp.concatenate([cos_p - sin_q, -(sin_p + cos_q)], 2)

def inverse(spectra, cos_table, sin_table):
    number = spectra.shape[0]
    upper = jnp.concatenate([cos_table.T, sin_table.T], 1)
    lower = jnp.concatenate([-sin_table.T, cos_table.T], 1)
    widen = jnp.concatenate([upper, lower], 0)
    section_one = jnp.dot(spectra.reshape(number * KF, 2 * KF), widen, preferred_element_type=jnp.float32)
    section_one = section_one.astype(jnp.bfloat16).reshape(number, KF, 2 * PIX)
    restacked = jnp.concatenate([section_one[:, :, :PIX], section_one[:, :, PIX:]], 1)
    combine = jnp.concatenate([cos_table, -sin_table], 1)
    return jnp.einsum('yk,nkx->nyx', combine.astype(jnp.float32), restacked.astype(jnp.float32))

def ctf_planes(bin_values):
    freq_index = jnp.arange(KF, dtype=jnp.int32) - KF // 2
    radius = (freq_index[:, None] * freq_index[:, None] + freq_index[None, :] * freq_index[None, :]).astype(jnp.float32) / float(KF // 2 * (KF // 2))
    factor = ctf_scale * (1.0 + bin_values / BINS)
    return -jnp.sin(factor[:, None, None] * radius[None, :, :] + amp_phase)

def slot_terms(spectra, chosen, ctf, occupied, cos_table, sin_table):
    image_re = spectra[:, :, :KF].astype(jnp.float32)
    image_im = spectra[:, :, KF:].astype(jnp.float32)
    ref_re = chosen[:, :, :KF].astype(jnp.float32)
    ref_im = chosen[:, :, KF:].astype(jnp.float32)
    cross_re = ctf * (ref_re * image_re + ref_im * image_im)
    cross_im = ctf * (ref_re * image_im - ref_im * image_re)
    cross_term = jnp.concatenate([cross_re, cross_im], 2).astype(jnp.bfloat16)
    ref_power = lax.optimization_barrier(jnp.sum(ctf * ctf * (ref_re * ref_re + ref_im * ref_im), axis=(1, 2)))
    image_power = lax.optimization_barrier(jnp.sum(image_re * image_re + image_im * image_im, axis=(1, 2)))
    scores = inverse(cross_term, cos_table, sin_table) * (PIX / jnp.sqrt(ref_power * image_power + 1e-06))[:, None, None]
    weights = jnp.exp(sharpness * (scores - 1.0))
    posterior = (weights / lax.optimization_barrier(jnp.sum(weights, axis=(1, 2), keepdims=True))).astype(jnp.bfloat16)
    shifts = forward(posterior, cos_table, sin_table)
    shift_re = shifts[:, :, :KF]
    shift_im = shifts[:, :, KF:]
    data_re = PIX * ctf * (shift_re * image_re + shift_im * image_im)
    data_im = PIX * ctf * (shift_re * image_im - shift_im * image_re)
    return jnp.concatenate([data_re, data_im, occupied[:, None, None] * ctf * ctf], 2)

def shell_index(cell_ids):
    coord_x = cell_ids // KF - KF // 2
    coord_y = cell_ids % KF - KF // 2
    depth_pos = jnp.arange(KF, dtype=jnp.int32) - KF // 2
    radius_sq = (coord_x * coord_x + coord_y * coord_y)[:, None] + (depth_pos * depth_pos)[None, :]
    bounds = jnp.arange(1, SHELLS, dtype=jnp.int32)
    return lax.optimization_barrier(jnp.sum(((bounds * bounds)[None, None, :] <= radius_sq[:, :, None]).astype(jnp.int32), axis=2)).astype(jnp.int32)

def reference(images, references, image_owner, image_class, defocus_bin, slice_cells):
    cos_table, sin_table = dft_tables()
    ref_spectra = forward(references.reshape(2 * CLASSES, PIX, PIX), cos_table, sin_table).astype(jnp.bfloat16)
    labels = jnp.arange(IMAGES, dtype=jnp.int32) // (IMAGES // 2) * CLASSES + image_owner[:, 0] * CLS_DEV + image_class
    images_per_block = 16
    blocks = IMAGES // images_per_block

    def accumulate(totals, block_index):
        offset = (block_index * images_per_block).astype(jnp.int32)
        planes = lax.dynamic_slice_in_dim(images, offset, images_per_block, 0)
        label_block = lax.dynamic_slice_in_dim(labels, offset, images_per_block, 0)
        bin_values = lax.dynamic_slice_in_dim(defocus_bin, offset, images_per_block, 0).astype(jnp.float32)
        spectra = forward(planes, cos_table, sin_table).astype(jnp.bfloat16)
        chosen = jnp.take(ref_spectra, label_block, axis=0)
        occupied = jnp.ones((images_per_block,), jnp.float32)
        terms = slot_terms(spectra, chosen, ctf_planes(bin_values), occupied, cos_table, sin_table)
        member = (label_block[None, :] == jnp.arange(2 * CLASSES, dtype=jnp.int32)[:, None]).astype(jnp.float32)
        totals = totals + jnp.dot(member, terms.reshape(images_per_block, KF * 3 * KF), precision=lax.Precision.HIGHEST)
        return (totals, None)
    totals, _ = lax.scan(accumulate, jnp.zeros((2 * CLASSES, KF * 3 * KF), jnp.float32), jnp.arange(blocks, dtype=jnp.int32))
    totals = totals.reshape(2, CLASSES * KF, 3 * KF)
    flat_cells = slice_cells.reshape(CLASSES * KF)
    volume = jnp.stack([jax.ops.segment_sum(totals[0], flat_cells, num_segments=CELLS), jax.ops.segment_sum(totals[1], flat_cells, num_segments=CELLS)], 0)
    weight_cols = volume[:, :, 2 * KF:]
    wiener = volume[:, :, :2 * KF] / (jnp.concatenate([weight_cols, weight_cols], 2) + 1.0)
    shells = shell_index(jnp.arange(CELLS, dtype=jnp.int32))
    flat_shell = shells.reshape(CELLS * KF)
    half_a = wiener[0]
    half_b = wiener[1]
    cross_term = (half_a[:, :KF] * half_b[:, :KF] + half_a[:, KF:] * half_b[:, KF:]).reshape(CELLS * KF)
    power_a = (half_a[:, :KF] * half_a[:, :KF] + half_a[:, KF:] * half_a[:, KF:]).reshape(CELLS * KF)
    power_b = (half_b[:, :KF] * half_b[:, :KF] + half_b[:, KF:] * half_b[:, KF:]).reshape(CELLS * KF)
    corr_sum = jax.ops.segment_sum(cross_term, flat_shell, num_segments=SHELLS)
    sum_a = jax.ops.segment_sum(power_a, flat_shell, num_segments=SHELLS)
    sum_b = jax.ops.segment_sum(power_b, flat_shell, num_segments=SHELLS)
    shell_corr = corr_sum / jnp.maximum(jnp.sqrt(sum_a * sum_b), 1.0)
    positive = jnp.maximum(shell_corr, 0.0)
    shell_weight = jnp.sqrt(2.0 * positive / (1.0 + positive))
    voxel_weight = jnp.take(shell_weight, shells, axis=0)
    return wiener * jnp.concatenate([voxel_weight, voxel_weight], 1)[None, :, :]
```

```python
import functools
import math

import jax
import jax.numpy as jnp
import numpy as np
from jax import lax
from jax.experimental import pallas as pl
from jax.experimental.pallas import tpu as pltpu
from jax.sharding import PartitionSpec as P

PIX = 256
KF = 128
HK = 64
CLS_DEV = 2
BINS = 16
SHELLS = 64
NY, NZ, NX = 4, 8, 4
OWNERS = NY * NZ
ROWS = 144
PR = 80
PA = 48
GROUP = 4

sharpness = 40.0
ctf_scale = 6.0
amp_phase = 0.1

MESH = pl.DeviceIdType.MESH
BF = jnp.bfloat16
F32 = jnp.float32


def dft_tables():
    sample_pos = np.arange(PIX, dtype=np.int32)[:, None]
    freq_pos = np.arange(KF, dtype=np.int32)[None, :] - KF // 2
    angles = (sample_pos * freq_pos % PIX).astype(np.float32) * np.float32(2.0 * math.pi / PIX)
    scaling = np.float32(1.0 / math.sqrt(PIX))
    bf = jnp.bfloat16
    return (np.cos(angles) * scaling).astype(bf), (np.sin(angles) * scaling).astype(bf)


def ctf_table():
    freq = np.arange(KF, dtype=np.int32) - KF // 2
    radius = (freq[:, None] * freq[:, None] + freq[None, :] * freq[None, :]).astype(
        np.float32
    ) / np.float32(HK * HK)
    factor = (ctf_scale * (1.0 + np.arange(BINS) / BINS)).astype(np.float32)
    return -np.sin(factor[:, None, None] * radius[None] + np.float32(amp_phase)).astype(np.float32)


def expand_tables():
    turn = np.zeros((256, 256), np.float32)
    column = np.zeros((256, 256), np.float32)
    middle = np.zeros((256, 256), np.float32)
    for c in range(1, KF):
        turn[c, KF - c] = 1.0
        turn[KF + c, 2 * KF - c] = -1.0
    column[:KF, 0] = 1.0
    column[KF:, KF] = 1.0
    for c in range(HK + 1):
        middle[c, c] = 1.0
        middle[KF + c, KF + c] = 1.0
    for c in range(1, HK):
        middle[c, KF - c] = 1.0
        middle[KF + c, 2 * KF - c] = -1.0
    return np.concatenate([turn, column, middle], 0)


def row_turn():
    turn = np.zeros((HK, HK), np.float32)
    for r in range(1, HK):
        turn[r, HK - r] = 1.0
    return turn


def dot(a, b):
    return jnp.dot(a, b, preferred_element_type=F32)


def pick(chooser, rows):
    high = rows.astype(BF)
    return dot(chooser, high) + dot(chooser, (rows - high.astype(F32)).astype(BF))


def transform(plane, cs, cst):
    section = dot(plane, cs).astype(BF)
    both = dot(cst, section)
    real = both[:KF, :KF] - both[KF:, KF:]
    imag = -(both[KF:, :KF] + both[:KF, KF:])
    return real, imag


def left_over(part):
    low = part[HK:, :]
    row = lax.broadcasted_iota(jnp.int32, (HK, KF), 0)
    col = lax.broadcasted_iota(jnp.int32, (HK, KF), 1)
    line = jnp.sum(jnp.where((col == row + HK) & (row > 0), low[:, 0:1], 0.0), axis=0, keepdims=True)
    first = lax.broadcasted_iota(jnp.int32, (1, KF), 1) <= HK
    return jnp.where(first, low[0:1, :], line)


def lower_masks(rows):
    row = lax.broadcasted_iota(jnp.int32, (rows, 2 * KF), 0) % KF
    col = lax.broadcasted_iota(jnp.int32, (rows, 2 * KF), 1) % KF
    return (row > HK) & (col == row), (row == HK) & (col <= HK)


def here():
    half, cls, tile = lax.axis_index("half"), lax.axis_index("cls"), lax.axis_index("tile")
    y, z = cls // NZ, cls % NZ

    def at(dy=0, dz=0, dx=0):
        return (half, (y + dy) % NY * NZ + (z + dz) % NZ, (tile + dx) % NX)

    return half, y, z, tile, at


def remote(src, dst, send, recv, device):
    return pltpu.make_async_remote_copy(
        src_ref=src, dst_ref=dst, send_sem=send, recv_sem=recv, device_id=device, device_id_type=MESH
    )


def greet(devices):
    barrier = pltpu.get_barrier_semaphore()
    for device in devices:
        pl.semaphore_signal(barrier, inc=1, device_id=device, device_id_type=MESH)
    pl.semaphore_wait(barrier, len(devices))


GATHER_SEMS = 72


def gather_kernel(plane_ref, cs_ref, cst_ref, g_ref, own_ref, send_sem, recv_sem):
    _, y, z, tile, at = here()
    greet([at(dz=1), at(dz=-1), at(dy=1), at(dy=-1), at(dx=1), at(dx=-1)])
    line = lax.broadcasted_iota(jnp.int32, (16, KF), 0)
    tail_re = jnp.zeros((16, KF), F32)
    tail_im = jnp.zeros((16, KF), F32)
    for k in range(CLS_DEV):
        real, imag = transform(plane_ref[k], cs_ref[...], cst_ref[...])
        own_ref[k * HK : (k + 1) * HK, 0:KF] = real[:HK].astype(BF)
        own_ref[k * HK : (k + 1) * HK, KF : 2 * KF] = imag[:HK].astype(BF)
        tail_re = jnp.where(line == k, left_over(real), tail_re)
        tail_im = jnp.where(line == k, left_over(imag), tail_im)
    own_ref[128:144, 0:KF] = tail_re.astype(BF)
    own_ref[128:144, KF : 2 * KF] = tail_im.astype(BF)

    sent = []

    def copy(i, view, device):
        ref = g_ref.at[view]
        return remote(ref, ref, send_sem.at[i], recv_sem.at[i], device)

    def push(view, device):
        i = len(sent)
        out = copy(i, view, device)
        out.start()
        sent.append(out)
        return i

    def take(i, view):
        copy(i, view, at(dz=1)).wait_recv()

    def along(dx):
        return pl.ds(pl.multiple_of(PR + 16 * ((tile + dx) % NX), 16), 16)

    whole, front, back = pl.ds(0, PR), pl.ds(0, PA), pl.ds(PA, PR - PA)
    every, low, high = pl.ds(0, NZ), pl.ds(0, NZ // 2), pl.ds(NZ // 2, NZ // 2)
    mine = along(0)
    g_ref[y, z, whole, :] = own_ref[whole, :]
    g_ref[y, z, mine, :] = own_ref[mine, :]
    up, down = at(dz=1), at(dz=-1)
    north, south = at(dy=1), at(dy=-1)
    east, west = at(dx=1), at(dx=-1)
    yw, ye, yo = (y - 1) % NY, (y + 1) % NY, (y + 2) % NY

    r_up, r_down = push((y, z, mine), up), push((y, z, mine), down)
    p_up, p_down = push((y, z, whole), up), push((y, z, whole), down)
    waiting, last = [], []

    def cross(zz):
        waiting.append((zz, push((y, zz, whole), north), push((y, zz, whole), south)))

    def settle():
        zz, a, b = waiting.pop(0)
        take(a, (yw, zz, whole))
        fa = push((yw, zz, front), north)
        take(b, (ye, zz, whole))
        fb = push((ye, zz, back), south)
        last.append((zz, fa, fb))

    cross(z)
    for d in range(1, 5):
        zm, zp = (z - d) % NZ, (z + d) % NZ
        take(r_up, (y, zm, mine))
        if d < 4:
            r_up = push((y, zm, mine), up)
            take(r_down, (y, zp, mine))
        if d < 3:
            r_down = push((y, zp, mine), down)
        if d == 4:
            a, b = push((y, every, mine), north), push((y, every, mine), south)
        take(p_up, (y, zm, whole if d < 4 else front))
        if d < 4:
            p_up = push((y, zm, whole if d < 3 else front), up)
        take(p_down, (y, zp, whole if d < 4 else back))
        if d < 4:
            p_down = push((y, zp, whole if d < 3 else back), down)
            cross(zm)
        cross(zp)
        settle()

    def spread(yy):
        return yy, push((yy, every, mine), east), push((yy, every, mine), west)

    x_wait, x_last = [spread(y)], []

    def x_settle():
        yy, p, q = x_wait.pop(0)
        take(p, (yy, every, along(-1)))
        fp = push((yy, low, along(-1)), east)
        take(q, (yy, every, along(1)))
        fq = push((yy, high, along(1)), west)
        x_last.append((yy, fp, fq))

    take(a, (yw, every, mine))
    fa = push((yw, low, mine), north)
    x_wait.append(spread(yw))
    take(b, (ye, every, mine))
    fb = push((ye, high, mine), south)
    x_wait.append(spread(ye))
    settle()
    take(fa, (yo, low, mine))
    take(fb, (yo, high, mine))
    x_wait.append(spread(yo))
    while waiting or x_wait:
        if x_wait:
            x_settle()
        if waiting:
            settle()
    for zz, fa, fb in last:
        take(fa, (yo, zz, front))
        take(fb, (yo, zz, back))
    for yy, fp, fq in x_last:
        take(fp, (yy, low, along(2)))
        take(fq, (yy, high, along(2)))
    for out in sent:
        out.wait_send()


def image_kernel(
    owner_ref, class_ref, bin_ref, img_ref, refs_ref, ctf_ref, cs_ref, cst_ref, widen_ref,
    combine_ref, expand_ref, turn_ref, out_ref, acc_ref,
):
    step = pl.program_id(0)

    @pl.when(step == 0)
    def _():
        acc_ref[...] = jnp.zeros_like(acc_ref)

    cs, cst = cs_ref[...], cst_ref[...]
    diag, mid = lower_masks(KF)
    diag, mid = diag[HK:], mid[HK:]
    row8 = lax.broadcasted_iota(jnp.int32, (8, 2 * KF), 0)
    col8 = lax.broadcasted_iota(jnp.int32, (8, 2 * KF), 1)

    loaded = []
    for g in range(GROUP):
        n = step * GROUP + g
        o, k, b = owner_ref[n], class_ref[n], bin_ref[n]
        im_re, im_im = transform(img_ref[g], cs, cst)
        im_re, im_im = im_re.astype(BF).astype(F32), im_im.astype(BF).astype(F32)
        top = refs_ref[o, pl.ds(pl.multiple_of(k * HK, HK), HK), :]
        tail = refs_ref[o, 128:144, :].astype(F32)
        extra = jnp.where(k > 0, tail[1:2, :], tail[0:1, :])
        back = dot(top, expand_ref[0:256, :]).astype(BF)
        fill = jnp.concatenate(
            [jnp.where(diag, extra, 0.0).astype(BF), jnp.where(mid, extra, 0.0).astype(BF)], 1
        )
        low = dot(turn_ref[...], back) + dot(fill, expand_ref[256:768, :])
        full = jnp.concatenate([top.astype(F32), low], 0)
        ref_re, ref_im = full[:, :KF], full[:, KF:]
        ctf = ctf_ref[b]
        cross_re = ctf * (ref_re * im_re + ref_im * im_im)
        cross_im = ctf * (ref_re * im_im - ref_im * im_re)
        crossed = jnp.concatenate([cross_re, cross_im], 1).astype(BF)
        ref_power = jnp.sum(ctf * ctf * (ref_re * ref_re + ref_im * ref_im), keepdims=True)
        image_power = jnp.sum(im_re * im_re + im_im * im_im, keepdims=True)
        scale = (PIX * sharpness) / jnp.sqrt(ref_power * image_power + 1e-06)
        loaded.append((o, k, b, im_re, im_im, ctf, crossed, scale))
    ends = []
    for g in range(GROUP):
        o, k, b, im_re, im_im, ctf, crossed, scale = loaded[g]
        inner = dot(crossed, widen_ref[...]).astype(BF)
        stacked = jnp.concatenate([inner[:, :PIX], inner[:, PIX:]], 0)
        scores = dot(combine_ref[...], stacked)
        weights = jnp.exp(scores * scale - sharpness)
        total = jnp.sum(weights, keepdims=True)
        posterior = (weights * (1.0 / total)).astype(BF)
        sh_re, sh_im = transform(posterior, cs, cst)
        ctf = PIX * ctf
        data_re = ctf * (sh_re * im_re + sh_im * im_im)
        data_im = ctf * (sh_re * im_im - sh_im * im_re)
        ends.append((o, k, b, data_re, data_im))
    for g in range(GROUP):
        o, k, b, data_re, data_im = ends[g]
        rows = pl.ds(pl.multiple_of(k * HK, HK), HK)
        acc_ref[o, rows, 0:KF] += data_re[:HK]
        acc_ref[o, rows, KF : 2 * KF] += data_im[:HK]
        extra = jnp.concatenate([left_over(data_re), left_over(data_im)], 1)
        count = jnp.where((row8 == 2) & (col8 == k * BINS + b), 1.0, 0.0)
        acc_ref[o, 128:136, :] += jnp.where(row8 == k, extra, count)

    @pl.when(step == pl.num_programs(0) - 1)
    def _():
        out_ref[...] = acc_ref[...].astype(BF)


REDUCE_SEMS = 160
Z_ORDER = (4, 3, 5, 2, 6, 1, 7, 0)


def reduce_kernel(
    d_ref, ctf_ref, slot_ref, cell_ref, expand_ref, left_ref, o_ref,
    pin_p, pin_m, ps_p, ps_m, pr_p, pr_m, pz_s, pz_r, px_s, px_r,
    rin_p, rin_m, rs_p, rs_m, rr_p, rr_m, ry_s, ry_r, rz_s, rz_r, rx_s, rx_r,
    held, sb, rb, wz_s, wz_r, sz_s, sz_r, sy_s, sy_r, sx_s, sx_r, bins,
    send_sem, recv_sem,
):
    half, y, z, tile, at = here()
    cls = y * NZ + z
    north, south = at(dy=1), at(dy=-1)
    east, west = at(dx=1), at(dx=-1)
    twin = (1 - half, cls, tile)

    def owner_at(k):
        return (half, (cls + k) % OWNERS, tile)

    greet([owner_at(k) for k in range(1, OWNERS)] + [at(dx=k) for k in (1, 2, 3)] + [twin])
    sent = []

    def push(src, dst, device):
        i = len(sent)
        out = remote(src, dst, send_sem.at[i], recv_sem.at[i], device)
        out.start()
        sent.append(out)
        return i

    def take(i, dst):
        remote(dst, dst, send_sem.at[i], recv_sem.at[i], east).wait_recv()

    def along(dx):
        return pl.ds(pl.multiple_of(PR + 16 * ((tile + dx) % NX), 16), 16)

    def f(v):
        return v.astype(F32)

    yn, ys, yo = (y + 1) % NY, (y - 1) % NY, (y + 2) % NY
    front, back, whole = pl.ds(0, PA), pl.ds(PA, PR - PA), pl.ds(0, PR)
    every = pl.ds(0, NZ)
    first_p, first_r = {}, {}
    for n, j in enumerate(Z_ORDER):
        zz = (z + j) % NZ
        first_p[j] = (
            push(d_ref.at[yo, zz, front], pin_p.at[j], north),
            push(d_ref.at[yo, zz, back], pin_m.at[j], south),
        )
        if n % 2 == 0:
            yy = n // 2
            if yy < 2:
                first_r[yy] = push(d_ref.at[yy, every, along(2)], rin_p.at[yy], east)
            else:
                first_r[yy] = push(d_ref.at[yy, every, along(2)], rin_m.at[yy - 2], west)
    second_p, second_r = {}, {}
    for n, j in enumerate(Z_ORDER):
        zz = (z + j) % NZ
        a, b = first_p[j]
        take(a, pin_p.at[j])
        ps_p[j, 0:PA] = (f(d_ref[yn, zz, 0:PA]) + f(pin_p[j])).astype(BF)
        ps_p[j, PA:PR] = d_ref[yn, zz, PA:PR]
        a = push(ps_p.at[j], pr_p.at[j], north)
        take(b, pin_m.at[j])
        ps_m[j, 0:PA] = d_ref[ys, zz, 0:PA]
        ps_m[j, PA:PR] = (f(d_ref[ys, zz, PA:PR]) + f(pin_m[j])).astype(BF)
        b = push(ps_m.at[j], pr_m.at[j], south)
        second_p[j] = a, b
        if n % 2 == 0:
            yy = n // 2
            if yy < 2:
                take(first_r[yy], rin_p.at[yy])
                rs_p[yy] = (f(d_ref[yy, every, along(1)]) + f(rin_p[yy])).astype(BF)
                rs_m[yy] = d_ref[yy, every, along(-1)]
            else:
                take(first_r[yy], rin_m.at[yy - 2])
                rs_p[yy] = d_ref[yy, every, along(1)]
                rs_m[yy] = (f(d_ref[yy, every, along(-1)]) + f(rin_m[yy - 2])).astype(BF)
            second_r[yy] = (
                push(rs_p.at[yy], rr_p.at[yy], east),
                push(rs_m.at[yy], rr_m.at[yy], west),
            )
    third_p = {}
    for n, j in enumerate(Z_ORDER):
        zz = (z + j) % NZ
        a, b = second_p[j]
        take(a, pr_p.at[j])
        take(b, pr_m.at[j])
        pz_s[j] = (f(d_ref[y, zz, 0:PR]) + f(pr_p[j]) + f(pr_m[j])).astype(BF)
        if j:
            third_p[j] = push(pz_s.at[j], pz_r.at[j], at(dz=j))
        if n % 2 == 0:
            yy = n // 2
            a, b = second_r[yy]
            take(a, rr_p.at[yy])
            take(b, rr_m.at[yy])
            ry_s[yy] = (f(d_ref[yy, every, along(0)]) + f(rr_p[yy]) + f(rr_m[yy])).astype(BF)
    third_r = {k: push(ry_s.at[(y + k) % NY], ry_r.at[k], at(dy=k)) for k in (2, 1, 3)}
    total = f(ry_s[y])
    for k in (1, 2, 3):
        take(third_r[k], ry_r.at[k])
        total = total + f(ry_r[k])
    rz_s[...] = total.astype(BF)
    fourth_r = {j: push(rz_s.at[(z + j) % NZ], rz_r.at[j], at(dz=j)) for j in Z_ORDER[:-1]}
    total = f(pz_s[0])
    for j in range(1, NZ):
        take(third_p[j], pz_r.at[j])
        total = total + f(pz_r[j])
    px_s[...] = total
    fourth_p = {k: push(px_s, px_r.at[k], at(dx=k)) for k in (1, 2, 3)}
    total = f(rz_s[z])
    for j in range(1, NZ):
        take(fourth_r[j], rz_r.at[j])
        total = total + f(rz_r[j])
    rx_s[...] = total
    fifth_r = {k: push(rx_s, rx_r.at[k], at(dx=k)) for k in (1, 2, 3)}
    total = px_s[...]
    for k in (1, 2, 3):
        take(fourth_p[k], px_r.at[k])
        total = total + px_r[k]
    held[0:PR] = total
    held[along(0), :] = rx_s[...]
    for k in (1, 2, 3):
        take(fifth_r[k], rx_r.at[k])
        held[along(-k), :] = rx_r[k]

    sums = held[...]
    spread = pick(left_ref[...], sums)
    diag, mid = lower_masks(2 * KF)
    extra = spread[512:768]
    parts = jnp.concatenate(
        [spread[256:512], jnp.where(diag, extra, 0.0), jnp.where(mid, extra, 0.0)], 1
    )
    high = parts.astype(BF)
    rest = (parts - f(high)).astype(BF)
    data = spread[0:256] + dot(high, expand_ref[...]) + dot(rest, expand_ref[...])
    counts = sums[128:144]
    weights = []
    for k in range(CLS_DEV):
        weight = jnp.zeros((KF, KF), F32)
        for b in range(BINS):
            ctf = ctf_ref[b]
            weight = weight + counts[2:3, k * BINS + b : k * BINS + b + 1] * (ctf * ctf)
        weights.append(weight)
    weight = jnp.concatenate(weights, 0)
    place = lax.broadcasted_iota(jnp.int32, (OWNERS * 16, 2 * KF), 0)
    slot = slot_ref[...]
    packed = jnp.zeros((OWNERS * 16, KF), F32)
    for c, piece in enumerate((data[:, :KF], data[:, KF:], weight)):
        chooser = jnp.where(place == slot + 4 * c, 1.0, 0.0).astype(BF)
        packed = packed + pick(chooser, piece)
    sb[...] = packed.reshape(OWNERS, 16, KF)
    rb[cls] = sb[cls]
    used = pl.ds(0, 12)
    went = {
        k: push(sb.at[(cls + k) % OWNERS, used], rb.at[cls, used], owner_at(k)) for k in range(1, OWNERS)
    }
    for k in range(1, OWNERS):
        rb[(cls - k) % OWNERS, 12:16] = jnp.zeros((4, KF), F32)
        take(went[k], rb.at[(cls - k) % OWNERS, used])

    arrived = rb[...].reshape(OWNERS * 16, KF)
    cell = lax.broadcasted_iota(jnp.int32, (KF, OWNERS * 16), 0)
    kind = lax.broadcasted_iota(jnp.int32, (KF, OWNERS * 16), 1) % 16 // 4
    hit = cell == cell_ref[...]
    volume = [pick(jnp.where(hit & (kind == c), 1.0, 0.0).astype(BF), arrived) for c in range(3)]
    scale = 1.0 / (volume[2] + 1.0)
    w_re, w_im = volume[0] * scale, volume[1] * scale
    wz_s[:, 0:KF] = w_re.astype(BF)
    wz_s[:, KF : 2 * KF] = w_im.astype(BF)
    i = push(wz_s, wz_r, twin)
    d0 = lax.broadcasted_iota(jnp.int32, (KF, KF), 0) - HK
    d1 = lax.broadcasted_iota(jnp.int32, (KF, KF), 1) - HK
    plane = cls * NX + tile - HK
    radius = plane * plane + d0 * d0 + d1 * d1
    own = w_re * w_re + w_im * w_im
    take(i, wz_r)
    o_re, o_im = f(wz_r[:, 0:KF]), f(wz_r[:, KF : 2 * KF])
    both = w_re * o_re + w_im * o_im
    other = o_re * o_re + o_im * o_im

    for s in range(SHELLS):
        inside = radius >= s * s
        if s < SHELLS - 1:
            inside = inside & (radius < (s + 1) * (s + 1))
        for q, v in enumerate((both, own, other)):
            part = jnp.where(inside, v, 0.0).reshape(KF // 8, 8, KF)
            bins[q, s * 8 : s * 8 + 8, :] = jnp.sum(part, axis=0)
    line = lax.broadcasted_iota(jnp.int32, (8, KF), 0)
    ones = jnp.ones((8, KF), F32)
    group = lax.broadcasted_iota(jnp.int32, (SHELLS * 8, KF), 0) // 8
    group = jnp.where(group == lax.broadcasted_iota(jnp.int32, (SHELLS * 8, KF), 1), 1.0, 0.0)
    sums = jnp.zeros((8, KF), F32)
    for q in range(3):
        part = lax.dot_general(
            ones, bins[q], (((1,), (1,)), ((), ())), precision=lax.Precision.HIGHEST,
            preferred_element_type=F32,
        )
        part = jnp.dot(part, group, precision=lax.Precision.HIGHEST, preferred_element_type=F32)
        sums = jnp.where(line == q, part, sums)
    for s_ref, r_ref, devices in (
        (sz_s, sz_r, {j: at(dz=j) for j in Z_ORDER[:-1]}),
        (sy_s, sy_r, {k: at(dy=k) for k in (2, 1, 3)}),
        (sx_s, sx_r, {k: at(dx=k) for k in (2, 1, 3)}),
    ):
        s_ref[...] = sums
        tags = {k: push(s_ref, r_ref.at[k], device) for k, device in devices.items()}
        for k, tag in tags.items():
            take(tag, r_ref.at[k])
            sums = sums + r_ref[k]
    fsc = sums[0:1] / jnp.maximum(jnp.sqrt(sums[1:2] * sums[2:3]), 1.0)
    fsc = jnp.maximum(fsc, 0.0)
    gain = jnp.sqrt(2.0 * fsc / (1.0 + fsc))
    voxel = jnp.zeros((KF, KF), F32)
    for s in range(SHELLS):
        voxel = jnp.where(radius >= s * s, gain[:, s : s + 1], voxel)
    o_ref[0, :, 0:KF] = w_re * voxel
    o_ref[0, :, KF : 2 * KF] = w_im * voxel
    for out in sent:
        out.wait_send()


def left_table():
    table = np.zeros((768, ROWS), np.float32)
    for k in range(CLS_DEV):
        for r in range(KF):
            if r < HK:
                table[k * KF + r, k * HK + r] = 1.0
            elif r > HK:
                table[256 + k * KF + r, k * HK + KF - r] = 1.0
            table[512 + k * KF + r, 2 * HK + k] = 1.0
    return table


def routes(slice_cells):
    cls, tile = lax.axis_index("cls"), lax.axis_index("tile")
    cells = slice_cells.reshape(OWNERS, CLS_DEV * KF)
    block = cells // KF
    own = lax.dynamic_index_in_dim(block, cls, 0, keepdims=False)
    entry = jnp.arange(CLS_DEV * KF, dtype=jnp.int32)
    same = (own[:, None] == own[None, :]) & (entry[:, None] < entry[None, :])
    rank = jnp.sum(same.astype(jnp.int32), axis=0)
    slot = jnp.where(own % NX == tile, own // NX * 16 + rank, -4096)[None, :]
    mine = block == cls * NX + tile
    strict = jnp.asarray(np.triu(np.ones((256, 256), np.float32), 1), BF)
    before = dot(mine.astype(BF), strict).astype(jnp.int32)
    want = mine[:, None, :] & (before[:, None, :] == jnp.arange(4, dtype=jnp.int32)[None, :, None])
    cell = jnp.sum(jnp.where(want, cells[:, None, :] % KF + 1, 0), axis=2) - 1
    empty = jnp.full((OWNERS, 4), -1, jnp.int32)
    return slot, jnp.concatenate([cell, cell, cell, empty], 1).reshape(1, OWNERS * 16)


def shards(images, references, image_owner, image_class, defocus_bin, slice_cells):
    cos_table, sin_table = dft_tables()
    cs = jnp.asarray(np.concatenate([cos_table, sin_table], 1))
    cst = jnp.asarray(np.concatenate([cos_table.T, sin_table.T], 0))
    widen = jnp.asarray(
        np.concatenate(
            [
                np.concatenate([cos_table.T, sin_table.T], 1),
                np.concatenate([-sin_table.T, cos_table.T], 1),
            ],
            0,
        )
    )
    combine = jnp.asarray(np.concatenate([cos_table, -sin_table], 1))
    ctf = jnp.asarray(ctf_table())
    expand = jnp.asarray(expand_tables(), BF)
    turn = jnp.asarray(row_turn(), BF)
    left = jnp.asarray(left_table(), BF)
    local = images.shape[0]
    vmem = pl.BlockSpec(memory_space=pltpu.VMEM)
    dma = pltpu.SemaphoreType.DMA

    spectra = pl.pallas_call(
        gather_kernel,
        name="gather_references",
        out_shape=jax.ShapeDtypeStruct((NY, NZ, ROWS, 2 * KF), BF),
        in_specs=[vmem] * 3,
        out_specs=vmem,
        scratch_shapes=[
            pltpu.VMEM((ROWS, 2 * KF), BF), dma((GATHER_SEMS,)), dma((GATHER_SEMS,)),
        ],
        compiler_params=pltpu.CompilerParams(
            collective_id=0, has_side_effects=True, vmem_limit_bytes=32 << 20
        ),
    )(references[0], cs, cst)

    def fixed(shape):
        return pl.BlockSpec(shape, lambda i, *_: (0,) * len(shape))

    partial = pl.pallas_call(
        image_kernel,
        name="image_terms",
        out_shape=jax.ShapeDtypeStruct((OWNERS, ROWS, 2 * KF), BF),
        grid_spec=pltpu.PrefetchScalarGridSpec(
            num_scalar_prefetch=3,
            grid=(local // GROUP,),
            in_specs=[
                pl.BlockSpec((GROUP, PIX, PIX), lambda i, *_: (i, 0, 0)),
                fixed((OWNERS, ROWS, 2 * KF)),
                fixed((BINS, KF, KF)),
                fixed((PIX, 2 * KF)),
                fixed((2 * KF, PIX)),
                fixed((2 * KF, 2 * PIX)),
                fixed((PIX, 2 * KF)),
                fixed((768, 256)),
                fixed((HK, HK)),
            ],
            out_specs=fixed((OWNERS, ROWS, 2 * KF)),
            scratch_shapes=[pltpu.VMEM((OWNERS, ROWS, 2 * KF), F32)],
        ),
        compiler_params=pltpu.CompilerParams(
            dimension_semantics=("arbitrary",), vmem_limit_bytes=48 << 20
        ),
    )(
        image_owner[:, 0], image_class, defocus_bin, images,
        spectra.reshape(OWNERS, ROWS, 2 * KF), ctf, cs, cst, widen, combine, expand, turn,
    )

    slot, cell = routes(slice_cells)

    def buf(*shape):
        return pltpu.VMEM(shape, BF)

    wide = 2 * KF
    return pl.pallas_call(
        reduce_kernel,
        name="reduce_maps",
        out_shape=jax.ShapeDtypeStruct((1, KF, 2 * KF), F32),
        in_specs=[vmem] * 6,
        out_specs=vmem,
        scratch_shapes=[
            buf(NZ, PA, wide), buf(NZ, PR - PA, wide),
            buf(NZ, PR, wide), buf(NZ, PR, wide), buf(NZ, PR, wide), buf(NZ, PR, wide),
            buf(NZ, PR, wide), buf(NZ, PR, wide), pltpu.VMEM((PR, wide), F32), pltpu.VMEM((NX, PR, wide), F32),
            buf(2, NZ, 16, wide), buf(2, NZ, 16, wide),
            buf(NY, NZ, 16, wide), buf(NY, NZ, 16, wide), buf(NY, NZ, 16, wide), buf(NY, NZ, 16, wide),
            buf(NY, NZ, 16, wide), buf(NY, NZ, 16, wide), buf(NZ, 16, wide), buf(NZ, 16, wide),
            pltpu.VMEM((16, wide), F32), pltpu.VMEM((NX, 16, wide), F32),
            pltpu.VMEM((ROWS, wide), F32), pltpu.VMEM((OWNERS, 16, KF), F32), pltpu.VMEM((OWNERS, 16, KF), F32),
            buf(KF, wide), buf(KF, wide),
            pltpu.VMEM((8, KF), F32), pltpu.VMEM((NZ, 8, KF), F32),
            pltpu.VMEM((8, KF), F32), pltpu.VMEM((NY, 8, KF), F32),
            pltpu.VMEM((8, KF), F32), pltpu.VMEM((NX, 8, KF), F32), pltpu.VMEM((3, SHELLS * 8, KF), F32),
            dma((REDUCE_SEMS,)), dma((REDUCE_SEMS,)),
        ],
        compiler_params=pltpu.CompilerParams(
            collective_id=1, has_side_effects=True, vmem_limit_bytes=40 << 20
        ),
    )(partial.reshape(NY, NZ, ROWS, 2 * KF), ctf, slot, cell, expand, left)


def solution(mesh):
    placed = (
        P(("half", "cls", "tile"), None, None),
        P("half", "cls", None, None),
        P(("half", "cls", "tile"), None),
        P(("half", "cls", "tile")),
        P(("half", "cls", "tile")),
        P(),
    )
    return jax.shard_map(
        shards,
        mesh=mesh,
        in_specs=placed,
        out_specs=P("half", ("cls", "tile"), None),
        check_vma=False,
    )
```

```python
import functools
import math

import jax
import jax.numpy as jnp
import numpy as np
from jax import lax
from jax.experimental import pallas as pl
from jax.experimental.pallas import tpu as pltpu
from jax.sharding import PartitionSpec as P

PIX = 256
KF = 128
HK = 64
CLS_DEV = 2
BINS = 16
SHELLS = 64
NY, NZ, NX = 4, 8, 4
OWNERS = NY * NZ
ROWS = 144
PR = 80
PA = 48
GROUP = 8

sharpness = 40.0
ctf_scale = 6.0
amp_phase = 0.1

MESH = pl.DeviceIdType.MESH
BF = jnp.bfloat16
F32 = jnp.float32


def dft_tables():
    sample_pos = np.arange(PIX, dtype=np.int32)[:, None]
    freq_pos = np.arange(KF, dtype=np.int32)[None, :] - KF // 2
    angles = (sample_pos * freq_pos % PIX).astype(np.float32) * np.float32(2.0 * math.pi / PIX)
    scaling = np.float32(1.0 / math.sqrt(PIX))
    bf = jnp.bfloat16
    return (np.cos(angles) * scaling).astype(bf), (np.sin(angles) * scaling).astype(bf)


def ctf_table():
    freq = np.arange(KF, dtype=np.int32) - KF // 2
    radius = (freq[:, None] * freq[:, None] + freq[None, :] * freq[None, :]).astype(
        np.float32
    ) / np.float32(HK * HK)
    factor = (ctf_scale * (1.0 + np.arange(BINS) / BINS)).astype(np.float32)
    return -np.sin(factor[:, None, None] * radius[None] + np.float32(amp_phase)).astype(np.float32)


def expand_tables():
    turn = np.zeros((256, 256), np.float32)
    column = np.zeros((256, 256), np.float32)
    middle = np.zeros((256, 256), np.float32)
    for c in range(1, KF):
        turn[c, KF - c] = 1.0
        turn[KF + c, 2 * KF - c] = -1.0
    column[:KF, 0] = 1.0
    column[KF:, KF] = 1.0
    for c in range(HK + 1):
        middle[c, c] = 1.0
        middle[KF + c, KF + c] = 1.0
    for c in range(1, HK):
        middle[c, KF - c] = 1.0
        middle[KF + c, 2 * KF - c] = -1.0
    return np.concatenate([turn, column, middle], 0)


def row_turn():
    turn = np.zeros((HK, HK), np.float32)
    for r in range(1, HK):
        turn[r, HK - r] = 1.0
    return turn


def dot(a, b):
    return jnp.dot(a, b, preferred_element_type=F32)


def pick(chooser, rows):
    high = rows.astype(BF)
    return dot(chooser, high) + dot(chooser, (rows - high.astype(F32)).astype(BF))


def transform(plane, cs, cst):
    section = dot(plane, cs).astype(BF)
    both = dot(cst, section)
    real = both[:KF, :KF] - both[KF:, KF:]
    imag = -(both[KF:, :KF] + both[:KF, KF:])
    return real, imag


def left_over(part):
    low = part[HK:, :]
    row = lax.broadcasted_iota(jnp.int32, (HK, KF), 0)
    col = lax.broadcasted_iota(jnp.int32, (HK, KF), 1)
    line = jnp.sum(jnp.where((col == row + HK) & (row > 0), low[:, 0:1], 0.0), axis=0, keepdims=True)
    first = lax.broadcasted_iota(jnp.int32, (1, KF), 1) <= HK
    return jnp.where(first, low[0:1, :], line)


def lower_masks(rows):
    row = lax.broadcasted_iota(jnp.int32, (rows, 2 * KF), 0) % KF
    col = lax.broadcasted_iota(jnp.int32, (rows, 2 * KF), 1) % KF
    return (row > HK) & (col == row), (row == HK) & (col <= HK)


def here():
    half, cls, tile = lax.axis_index("half"), lax.axis_index("cls"), lax.axis_index("tile")
    y, z = cls // NZ, cls % NZ

    def at(dy=0, dz=0, dx=0):
        return (half, (y + dy) % NY * NZ + (z + dz) % NZ, (tile + dx) % NX)

    return half, y, z, tile, at


def remote(src, dst, send, recv, device):
    return pltpu.make_async_remote_copy(
        src_ref=src, dst_ref=dst, send_sem=send, recv_sem=recv, device_id=device, device_id_type=MESH
    )


def greet(devices):
    barrier = pltpu.get_barrier_semaphore()
    for device in devices:
        pl.semaphore_signal(barrier, inc=1, device_id=device, device_id_type=MESH)
    pl.semaphore_wait(barrier, len(devices))


GATHER_SEMS = 80


def gather_kernel(
    plane_any, table_any, g_ref, plane_ref, table_ref, own_ref, copy_sem, send_sem, recv_sem
):
    loads = [
        pltpu.make_async_copy(plane_any, plane_ref, copy_sem.at[0]),
        pltpu.make_async_copy(table_any, table_ref, copy_sem.at[1]),
    ]
    for load in loads:
        load.start()
    _, y, z, tile, at = here()
    greet([at(dz=k) for k in range(1, NZ)] + [at(dy=1), at(dy=-1), at(dx=1), at(dx=-1)])
    for load in loads:
        load.wait()
    line = lax.broadcasted_iota(jnp.int32, (16, KF), 0)
    tail_re = jnp.zeros((16, KF), F32)
    tail_im = jnp.zeros((16, KF), F32)
    for k in range(CLS_DEV):
        real, imag = transform(plane_ref[k], table_ref[0:PIX, :], table_ref[PIX : 2 * PIX, :])
        own_ref[k * HK : (k + 1) * HK, 0:KF] = real[:HK].astype(BF)
        own_ref[k * HK : (k + 1) * HK, KF : 2 * KF] = imag[:HK].astype(BF)
        tail_re = jnp.where(line == k, left_over(real), tail_re)
        tail_im = jnp.where(line == k, left_over(imag), tail_im)
    own_ref[128:144, 0:KF] = tail_re.astype(BF)
    own_ref[128:144, KF : 2 * KF] = tail_im.astype(BF)

    sent = []

    def copy(i, view, device):
        ref = g_ref.at[view]
        return remote(ref, ref, send_sem.at[i], recv_sem.at[i], device)

    def push(view, device):
        i = len(sent)
        out = copy(i, view, device)
        out.start()
        sent.append(out)
        return i

    def take(i, view):
        copy(i, view, at(dz=1)).wait_recv()

    def along(dx):
        return pl.ds(pl.multiple_of(PR + 16 * ((tile + dx) % NX), 16), 16)

    whole, front, back = pl.ds(0, PR), pl.ds(0, PA), pl.ds(PA, PR - PA)
    every, low, high = pl.ds(0, NZ), pl.ds(0, NZ // 2), pl.ds(NZ // 2, NZ // 2)
    mine = along(0)
    g_ref[y, z, whole, :] = own_ref[whole, :]
    g_ref[y, z, mine, :] = own_ref[mine, :]
    up, down = at(dz=1), at(dz=-1)
    north, south = at(dy=1), at(dy=-1)
    east, west = at(dx=1), at(dx=-1)
    yw, ye, yo = (y - 1) % NY, (y + 1) % NY, (y + 2) % NY

    r_tags = {j: push((y, z, mine), at(dz=j)) for j in (4, 3, 5, 2, 6, 1, 7)}
    p_up, p_down = push((y, z, whole), up), push((y, z, whole), down)
    waiting, last = [], []

    def cross(zz):
        waiting.append((zz, push((y, zz, whole), north), push((y, zz, whole), south)))

    def settle():
        zz, a, b = waiting.pop(0)
        take(a, (yw, zz, whole))
        fa = push((yw, zz, front), north)
        take(b, (ye, zz, whole))
        fb = push((ye, zz, back), south)
        last.append((zz, fa, fb))

    def spread(yy):
        return yy, push((yy, every, mine), east), push((yy, every, mine), west)

    x_wait, x_last = [], []

    def x_settle():
        yy, p, q = x_wait.pop(0)
        take(p, (yy, every, along(-1)))
        fp = push((yy, low, along(-1)), east)
        take(q, (yy, every, along(1)))
        fq = push((yy, high, along(1)), west)
        x_last.append((yy, fp, fq))

    cross(z)
    for j, tag in r_tags.items():
        take(tag, (y, (z - j) % NZ, mine))
    ra, rb = push((y, every, mine), north), push((y, every, mine), south)
    x_wait.append(spread(y))
    for d in range(1, 5):
        zm, zp = (z - d) % NZ, (z + d) % NZ
        take(p_up, (y, zm, whole if d < 4 else front))
        if d < 4:
            p_up = push((y, zm, whole if d < 3 else front), up)
        take(p_down, (y, zp, whole if d < 4 else back))
        if d < 4:
            p_down = push((y, zp, whole if d < 3 else back), down)
            cross(zm)
        cross(zp)
        if d == 1:
            take(ra, (yw, every, mine))
            fa = push((yw, low, mine), north)
            x_wait.append(spread(yw))
            take(rb, (ye, every, mine))
            fb = push((ye, high, mine), south)
            x_wait.append(spread(ye))
        elif d == 2:
            take(fa, (yo, low, mine))
            take(fb, (yo, high, mine))
            x_wait.append(spread(yo))
        else:
            x_settle()
        settle()
    while waiting or x_wait:
        if waiting:
            settle()
        if x_wait:
            x_settle()
    for zz, fa, fb in last:
        take(fa, (yo, zz, front))
        take(fb, (yo, zz, back))
    for yy, fp, fq in x_last:
        take(fp, (yy, low, along(2)))
        take(fq, (yy, high, along(2)))
    for out in sent:
        out.wait_send()


def image_kernel(
    owner_ref, class_ref, bin_ref, img_ref, refs_ref, ctf_ref, cs_ref, cst_ref, widen_ref,
    combine_ref, expand_ref, turn_ref, out_ref, acc_ref,
):
    step = pl.program_id(0)

    @pl.when(step == 0)
    def _():
        acc_ref[...] = jnp.zeros_like(acc_ref)

    cs, cst = cs_ref[...], cst_ref[...]
    diag, mid = lower_masks(KF)
    diag, mid = diag[HK:], mid[HK:]
    row8 = lax.broadcasted_iota(jnp.int32, (8, 2 * KF), 0)
    col8 = lax.broadcasted_iota(jnp.int32, (8, 2 * KF), 1)

    def halves(section):
        both = dot(cst, section)
        return both[:KF, :KF] - both[KF:, KF:], -(both[KF:, :KF] + both[:KF, KF:])

    section = dot(img_ref[...].reshape(GROUP * PIX, PIX), cs).astype(BF)
    which = [(owner_ref[step * GROUP + g], class_ref[step * GROUP + g], bin_ref[step * GROUP + g]) for g in range(GROUP)]
    tops = [refs_ref[o, pl.ds(pl.multiple_of(k * HK, HK), HK), :] for o, k, _ in which]
    backs = dot(jnp.concatenate(tops, 0), expand_ref[0:256, :]).astype(BF)
    fills = []
    for o, k, _ in which:
        tail = refs_ref[o, 128:144, :].astype(F32)
        extra = jnp.where(k > 0, tail[1:2, :], tail[0:1, :])
        fills.append(jnp.concatenate(
            [jnp.where(diag, extra, 0.0).astype(BF), jnp.where(mid, extra, 0.0).astype(BF)], 1
        ))
    filled = dot(jnp.concatenate(fills, 0), expand_ref[256:768, :])
    loaded, crosses = [], []
    for g in range(GROUP):
        o, k, b = which[g]
        im_re, im_im = halves(section[g * PIX : (g + 1) * PIX])
        im_re, im_im = im_re.astype(BF).astype(F32), im_im.astype(BF).astype(F32)
        low = dot(turn_ref[...], backs[g * HK : (g + 1) * HK]) + filled[g * HK : (g + 1) * HK]
        full = jnp.concatenate([tops[g].astype(F32), low], 0)
        ref_re, ref_im = full[:, :KF], full[:, KF:]
        ctf = ctf_ref[b]
        cross_re = ctf * (ref_re * im_re + ref_im * im_im)
        cross_im = ctf * (ref_re * im_im - ref_im * im_re)
        crosses.append(jnp.concatenate([cross_re, cross_im], 1).astype(BF))
        ref_power = jnp.sum(ctf * ctf * (ref_re * ref_re + ref_im * ref_im), keepdims=True)
        image_power = jnp.sum(im_re * im_re + im_im * im_im, keepdims=True)
        scale = (PIX * sharpness) / jnp.sqrt(ref_power * image_power + 1e-06)
        loaded.append((im_re, im_im, scale))
    inner = dot(jnp.concatenate(crosses, 0), widen_ref[...]).astype(BF)
    posteriors = []
    for g in range(GROUP):
        part = inner[g * KF : (g + 1) * KF]
        stacked = jnp.concatenate([part[:, :PIX], part[:, PIX:]], 0)
        scores = dot(combine_ref[...], stacked)
        weights = jnp.exp(scores * loaded[g][2] - sharpness)
        total = jnp.sum(weights, keepdims=True)
        posteriors.append((weights * (1.0 / total)).astype(BF))
    section = dot(jnp.concatenate(posteriors, 0), cs).astype(BF)
    for g in range(GROUP):
        o, k, b = which[g]
        im_re, im_im, _ = loaded[g]
        sh_re, sh_im = halves(section[g * PIX : (g + 1) * PIX])
        ctf = PIX * ctf_ref[b]
        data_re = ctf * (sh_re * im_re + sh_im * im_im)
        data_im = ctf * (sh_re * im_im - sh_im * im_re)
        rows = pl.ds(pl.multiple_of(k * HK, HK), HK)
        acc_ref[o, rows, 0:KF] += data_re[:HK]
        acc_ref[o, rows, KF : 2 * KF] += data_im[:HK]
        extra = jnp.concatenate([left_over(data_re), left_over(data_im)], 1)
        count = jnp.where((row8 == 2) & (col8 == k * BINS + b), 1.0, 0.0)
        acc_ref[o, 128:136, :] += jnp.where(row8 == k, extra, count)

    @pl.when(step == pl.num_programs(0) - 1)
    def _():
        out_ref[...] = acc_ref[...].astype(BF)


REDUCE_SEMS = 160
Z_ORDER = (4, 3, 5, 2, 6, 1, 7, 0)


def routes(cells, cls, tile):
    cells = cells.astype(F32)
    row = lax.broadcasted_iota(jnp.int32, (OWNERS, 2 * OWNERS), 0)
    col = lax.broadcasted_iota(jnp.int32, (OWNERS, 2 * OWNERS), 1)
    pair = [
        pick(jnp.where(col == 2 * row + k, 1.0, 0.0).astype(BF), cells) for k in range(CLS_DEV)
    ]
    cells = jnp.concatenate(pair, 1).astype(jnp.int32)
    block = lax.shift_right_arithmetic(cells, 7)
    inner = (cells - block * KF + 1).astype(F32)
    first = lax.broadcasted_iota(jnp.int32, (256, 256), 0)
    second = lax.broadcasted_iota(jnp.int32, (256, 256), 1)
    mine = block == cls * NX + tile
    strict = jnp.where(first < second, 1.0, 0.0).astype(BF)
    before = dot(jnp.where(mine, 1.0, 0.0).astype(BF), strict)
    owner = lax.broadcasted_iota(jnp.int32, (OWNERS, OWNERS * 16), 0)
    lane = lax.broadcasted_iota(jnp.int32, (OWNERS, OWNERS * 16), 1)
    here_ = (lax.shift_right_arithmetic(lane, 4) == owner) & ((lane & 15) < 12)
    table = jnp.zeros((OWNERS, OWNERS * 16), F32)
    for r in range(4):
        cell = jnp.sum(jnp.where(mine & (before == r), inner, 0.0), axis=1, keepdims=True)
        table = jnp.where(here_ & ((lane & 3) == r), cell, table)
    cell = (jnp.sum(table, axis=0, keepdims=True) - 1.0).astype(jnp.int32)
    owner = lax.broadcasted_iota(jnp.int32, (OWNERS, 256), 0)
    own = jnp.sum(jnp.where(owner == cls, block.astype(F32), 0.0), axis=0, keepdims=True)
    turned = jnp.sum(jnp.where(first == second, own, 0.0), axis=1, keepdims=True)
    same = jnp.where((turned == own) & (first < second), 1.0, 0.0)
    rank = jnp.sum(same, axis=0, keepdims=True).astype(jnp.int32)
    own = own.astype(jnp.int32)
    slot = lax.shift_right_arithmetic(own, 2) * 16 + rank
    return jnp.where((own & 3) == tile, slot, -4096), cell


def reduce_kernel(
    d_ref, ctf_ref, cells_ref, expand_any, left_any, o_ref,
    expand_ref, left_ref, pin_p, pin_m, ps_p, ps_m, pr_p, pr_m, pz_s, pz_r, px_s, px_r,
    rin_p, rin_m, rs_p, rs_m, rr_p, rr_m, ry_s, ry_r, rz_s, rz_r, rx_s, rx_r,
    held, sb, rb, wz_s, wz_r, sz_s, sz_r, sx_s, sx_r, bins,
    copy_sem, send_sem, recv_sem,
):
    half, y, z, tile, at = here()
    cls = y * NZ + z
    north, south = at(dy=1), at(dy=-1)
    east, west = at(dx=1), at(dx=-1)
    twin = (1 - half, cls, tile)

    def owner_at(k):
        return (half, (cls + k) % OWNERS, tile)

    tables = [
        pltpu.make_async_copy(expand_any, expand_ref, copy_sem.at[0]),
        pltpu.make_async_copy(left_any, left_ref, copy_sem.at[1]),
    ]
    for table in tables:
        table.start()
    plane_peers = {
        (dy, dx): at(dy=dy, dx=dx) for dy in (2, 1, 3, 0) for dx in (2, 1, 3, 0) if dy or dx
    }
    greet(
        [owner_at(k) for k in range(1, OWNERS)]
        + [device for (dy, dx), device in plane_peers.items() if dx]
        + [twin]
    )
    sent = []

    def push(src, dst, device):
        i = len(sent)
        out = remote(src, dst, send_sem.at[i], recv_sem.at[i], device)
        out.start()
        sent.append(out)
        return i

    def take(i, dst):
        remote(dst, dst, send_sem.at[i], recv_sem.at[i], east).wait_recv()

    def along(dx):
        return pl.ds(pl.multiple_of(PR + 16 * ((tile + dx) % NX), 16), 16)

    def f(v):
        return v.astype(F32)

    yn, ys, yo = (y + 1) % NY, (y - 1) % NY, (y + 2) % NY
    front, back = pl.ds(0, PA), pl.ds(PA, PR - PA)
    every = pl.ds(0, NZ)
    first_p, first_r = {}, {}
    for n, j in enumerate(Z_ORDER):
        zz = (z + j) % NZ
        if n < NY:
            if n < 2:
                first_r[n] = push(d_ref.at[n, every, along(2)], rin_p.at[n], east)
            else:
                first_r[n] = push(d_ref.at[n, every, along(2)], rin_m.at[n - 2], west)
        first_p[j] = (
            push(d_ref.at[yo, zz, front], pin_p.at[j], north),
            push(d_ref.at[yo, zz, back], pin_m.at[j], south),
        )
    plain_p, plain_r = {}, {}
    for n, j in enumerate(Z_ORDER):
        zz = (z + j) % NZ
        if n < NY:
            if n < 2:
                plain_r[n] = push(d_ref.at[n, every, along(-1)], rr_m.at[n], west)
            else:
                plain_r[n] = push(d_ref.at[n, every, along(1)], rr_p.at[n], east)
        plain_p[j] = (
            push(d_ref.at[yn, zz, back], pr_p.at[j, back], north),
            push(d_ref.at[ys, zz, front], pr_m.at[j, front], south),
        )

    slot, cell = routes(cells_ref[...], cls, tile)
    place = lax.broadcasted_iota(jnp.int32, (OWNERS * 16, 2 * KF), 0)
    chooser = jnp.concatenate(
        [jnp.where(place == slot + 4 * c, 1.0, 0.0).astype(BF) for c in range(3)], 1
    )

    second_p, second_r = {}, {}
    for n, j in enumerate(Z_ORDER):
        zz = (z + j) % NZ
        if n < NY:
            if n < 2:
                take(first_r[n], rin_p.at[n])
                rs_p[n] = (f(d_ref[n, every, along(1)]) + f(rin_p[n])).astype(BF)
                second_r[n] = push(rs_p.at[n], rr_p.at[n], east)
            else:
                take(first_r[n], rin_m.at[n - 2])
                rs_m[n - 2] = (f(d_ref[n, every, along(-1)]) + f(rin_m[n - 2])).astype(BF)
                second_r[n] = push(rs_m.at[n - 2], rr_m.at[n], west)
        a, b = first_p[j]
        take(a, pin_p.at[j])
        ps_p[j] = (f(d_ref[yn, zz, front]) + f(pin_p[j])).astype(BF)
        a = push(ps_p.at[j], pr_p.at[j, front], north)
        take(b, pin_m.at[j])
        ps_m[j] = (f(d_ref[ys, zz, back]) + f(pin_m[j])).astype(BF)
        b = push(ps_m.at[j], pr_m.at[j, back], south)
        second_p[j] = a, b

    third_p = {}

    def settle(j):
        zz = (z + j) % NZ
        a, b = plain_p[j]
        take(a, pr_p.at[j, back])
        take(b, pr_m.at[j, front])
        a, b = second_p[j]
        take(a, pr_p.at[j, front])
        take(b, pr_m.at[j, back])
        pz_s[j] = (f(d_ref[y, zz, pl.ds(0, PR)]) + f(pr_p[j]) + f(pr_m[j])).astype(BF)
        if j:
            third_p[j] = push(pz_s.at[j], pz_r.at[j], at(dz=j))

    for n, j in enumerate(Z_ORDER[:4]):
        settle(j)
        take(second_r[n], (rr_p if n < 2 else rr_m).at[n])
        take(plain_r[n], (rr_m if n < 2 else rr_p).at[n])
        ry_s[n] = (f(d_ref[n, every, along(0)]) + f(rr_p[n]) + f(rr_m[n])).astype(BF)
    third_r = {k: push(ry_s.at[(y + k) % NY], ry_r.at[k], at(dy=k)) for k in (2, 1, 3)}
    for j in Z_ORDER[4:6]:
        settle(j)
    total = f(ry_s[y])
    for k in (1, 2, 3):
        take(third_r[k], ry_r.at[k])
        total = total + f(ry_r[k])
    rz_s[...] = total.astype(BF)
    fourth_r = {j: push(rz_s.at[(z + j) % NZ], rz_r.at[j], at(dz=j)) for j in Z_ORDER[:-1]}
    for j in Z_ORDER[6:]:
        settle(j)

    d0 = lax.broadcasted_iota(jnp.int32, (KF, KF), 0) - HK
    d1 = lax.broadcasted_iota(jnp.int32, (KF, KF), 1) - HK
    plane = cls * NX + tile - HK
    radius = plane * plane + d0 * d0 + d1 * d1
    shell = jnp.zeros((KF, KF), jnp.int32)
    for s in range(1, SHELLS):
        shell = jnp.where(radius >= s * s, s, shell)

    total = f(rz_s[z])
    for j in range(1, NZ):
        take(fourth_r[j], rz_r.at[j])
        total = total + f(rz_r[j])
    rx_s[...] = total
    fifth_r = {k: push(rx_s, rx_r.at[k], at(dx=k)) for k in (2, 1, 3)}
    total = f(pz_s[0])
    for j in range(1, NZ):
        take(third_p[j], pz_r.at[j])
        total = total + f(pz_r[j])
    px_s[...] = total
    fourth_p = {k: push(px_s, px_r.at[k], at(dx=k)) for k in (2, 1, 3)}
    held[along(0), :] = rx_s[...]
    for k in (1, 2, 3):
        take(fifth_r[k], rx_r.at[k])
        held[along(-k), :] = rx_r[k]
    counts = held[128:144]
    weights = []
    for k in range(CLS_DEV):
        weight = jnp.zeros((KF, KF), F32)
        for b in range(BINS):
            ctf = ctf_ref[b]
            weight = weight + counts[2:3, k * BINS + b : k * BINS + b + 1] * (ctf * ctf)
        weights.append(weight)
    for table in tables:
        table.wait()
    total = px_s[...]
    for k in (1, 2, 3):
        take(fourth_p[k], px_r.at[k])
        total = total + px_r[k]
    held[0:PR] = total

    sums = held[...]
    spread = pick(left_ref[...], sums)
    diag, mid = lower_masks(2 * KF)
    extra = spread[512:768]
    parts = jnp.concatenate(
        [spread[256:512], jnp.where(diag, extra, 0.0), jnp.where(mid, extra, 0.0)], 1
    )
    high = parts.astype(BF)
    rest = (parts - f(high)).astype(BF)
    data = spread[0:256] + dot(high, expand_ref[...]) + dot(rest, expand_ref[...])
    packed = pick(chooser, jnp.concatenate([data[:, :KF], data[:, KF:]] + weights, 0))
    sb[...] = packed.reshape(OWNERS, 16, KF)
    rb[cls] = sb[cls]
    used = pl.ds(0, 12)
    went = {
        k: push(sb.at[(cls + k) % OWNERS, used], rb.at[cls, used], owner_at(k)) for k in range(1, OWNERS)
    }
    place = lax.broadcasted_iota(jnp.int32, (KF, OWNERS * 16), 0)
    kind = lax.shift_right_arithmetic(
        lax.broadcasted_iota(jnp.int32, (KF, OWNERS * 16), 1) & 15, 2
    )
    hit = place == cell
    hits = jnp.concatenate(
        [jnp.where(hit & (kind == c), 1.0, 0.0).astype(BF) for c in range(3)], 0
    )
    for k in range(1, OWNERS):
        rb[(cls - k) % OWNERS, 12:16] = jnp.zeros((4, KF), F32)
    for k in range(1, OWNERS):
        take(went[k], rb.at[(cls - k) % OWNERS, used])

    volume = pick(hits, rb[...].reshape(OWNERS * 16, KF))
    scale = 1.0 / (volume[2 * KF :] + 1.0)
    w_re, w_im = volume[:KF] * scale, volume[KF : 2 * KF] * scale
    wz_s[:, 0:KF] = w_re.astype(BF)
    wz_s[:, KF : 2 * KF] = w_im.astype(BF)
    i = push(wz_s, wz_r, twin)

    def collect(q, v):
        for s in range(SHELLS):
            part = jnp.where(shell == s, v, 0.0).reshape(KF // 8, 8, KF)
            bins[q, s * 8 : s * 8 + 8, :] = jnp.sum(part, axis=0)

    collect(1, w_re * w_re + w_im * w_im)
    take(i, wz_r)
    o_re, o_im = f(wz_r[:, 0:KF]), f(wz_r[:, KF : 2 * KF])
    collect(0, w_re * o_re + w_im * o_im)
    collect(2, o_re * o_re + o_im * o_im)
    line = lax.broadcasted_iota(jnp.int32, (8, KF), 0)
    ones = jnp.ones((8, KF), F32)
    group = lax.broadcasted_iota(jnp.int32, (SHELLS * 8, KF), 0) // 8
    group = jnp.where(group == lax.broadcasted_iota(jnp.int32, (SHELLS * 8, KF), 1), 1.0, 0.0)
    sums = jnp.zeros((8, KF), F32)
    for q in range(3):
        part = lax.dot_general(
            ones, bins[q], (((1,), (1,)), ((), ())), precision=lax.Precision.HIGHEST,
            preferred_element_type=F32,
        )
        part = jnp.dot(part, group, precision=lax.Precision.HIGHEST, preferred_element_type=F32)
        sums = jnp.where(line == q, part, sums)
    sz_s[...] = sums
    tags = {j: push(sz_s, sz_r.at[j], at(dz=j)) for j in Z_ORDER[:-1]}
    for j, tag in tags.items():
        take(tag, sz_r.at[j])
        sums = sums + sz_r[j]
    sx_s[...] = sums
    tags = {k: push(sx_s, sx_r.at[k[0], k[1]], device) for k, device in plane_peers.items()}
    for k, tag in tags.items():
        take(tag, sx_r.at[k[0], k[1]])
        sums = sums + sx_r[k[0], k[1]]
    fsc = sums[0:1] / jnp.maximum(jnp.sqrt(sums[1:2] * sums[2:3]), 1.0)
    fsc = jnp.maximum(fsc, 0.0)
    gain = jnp.sqrt(2.0 * fsc / (1.0 + fsc))
    voxel = jnp.zeros((KF, KF), F32)
    for s in range(SHELLS):
        voxel = jnp.where(shell == s, gain[:, s : s + 1], voxel)
    o_ref[0, :, 0:KF] = w_re * voxel
    o_ref[0, :, KF : 2 * KF] = w_im * voxel
    for out in sent:
        out.wait_send()


def left_table():
    table = np.zeros((768, ROWS), np.float32)
    for k in range(CLS_DEV):
        for r in range(KF):
            if r < HK:
                table[k * KF + r, k * HK + r] = 1.0
            elif r > HK:
                table[256 + k * KF + r, k * HK + KF - r] = 1.0
            table[512 + k * KF + r, 2 * HK + k] = 1.0
    return table


def shards(images, references, image_owner, image_class, defocus_bin, slice_cells):
    cos_table, sin_table = dft_tables()
    cs = jnp.asarray(np.concatenate([cos_table, sin_table], 1))
    cst = jnp.asarray(np.concatenate([cos_table.T, sin_table.T], 0))
    both = jnp.asarray(
        np.concatenate(
            [np.concatenate([cos_table, sin_table], 1), np.concatenate([cos_table.T, sin_table.T], 0)], 0
        )
    )
    widen = jnp.asarray(
        np.concatenate(
            [
                np.concatenate([cos_table.T, sin_table.T], 1),
                np.concatenate([-sin_table.T, cos_table.T], 1),
            ],
            0,
        )
    )
    combine = jnp.asarray(np.concatenate([cos_table, -sin_table], 1))
    ctf = jnp.asarray(ctf_table())
    expand = jnp.asarray(expand_tables(), BF)
    turn = jnp.asarray(row_turn(), BF)
    left = jnp.asarray(left_table(), BF)
    local = images.shape[0]
    vmem = pl.BlockSpec(memory_space=pltpu.VMEM)
    anywhere = pl.BlockSpec(memory_space=pltpu.HBM)
    dma = pltpu.SemaphoreType.DMA

    spectra = pl.pallas_call(
        gather_kernel,
        name="gather_references",
        out_shape=jax.ShapeDtypeStruct((NY, NZ, ROWS, 2 * KF), BF),
        in_specs=[anywhere] * 2,
        out_specs=vmem,
        scratch_shapes=[
            pltpu.VMEM((CLS_DEV, PIX, PIX), BF), pltpu.VMEM((2 * PIX, 2 * KF), BF),
            pltpu.VMEM((ROWS, 2 * KF), BF), dma((2,)), dma((GATHER_SEMS,)), dma((GATHER_SEMS,)),
        ],
        compiler_params=pltpu.CompilerParams(
            collective_id=0, has_side_effects=True, vmem_limit_bytes=44 << 20
        ),
    )(references[0], both)

    partial = pl.pallas_call(
        image_kernel,
        name="image_terms",
        out_shape=jax.ShapeDtypeStruct((OWNERS, ROWS, 2 * KF), BF),
        grid_spec=pltpu.PrefetchScalarGridSpec(
            num_scalar_prefetch=3,
            grid=(local // GROUP,),
            in_specs=[
                pl.BlockSpec((GROUP, PIX, PIX), lambda i, *_: (i, 0, 0)),
                *[vmem] * 8,
            ],
            out_specs=vmem,
            scratch_shapes=[pltpu.VMEM((OWNERS, ROWS, 2 * KF), F32)],
        ),
        compiler_params=pltpu.CompilerParams(
            dimension_semantics=("arbitrary",), vmem_limit_bytes=44 << 20
        ),
    )(
        image_owner[:, 0], image_class, defocus_bin, images,
        spectra.reshape(OWNERS, ROWS, 2 * KF), ctf, cs, cst, widen, combine, expand, turn,
    )

    def buf(*shape):
        return pltpu.VMEM(shape, BF)

    wide = 2 * KF
    return pl.pallas_call(
        reduce_kernel,
        name="reduce_maps",
        out_shape=jax.ShapeDtypeStruct((1, KF, 2 * KF), F32),
        in_specs=[vmem] * 3 + [anywhere] * 2,
        out_specs=vmem,
        scratch_shapes=[
            buf(768, 256), buf(768, ROWS), buf(NZ, PA, wide), buf(NZ, PR - PA, wide),
            buf(NZ, PA, wide), buf(NZ, PR - PA, wide), buf(NZ, PR, wide), buf(NZ, PR, wide),
            buf(NZ, PR, wide), buf(NZ, PR, wide),
            pltpu.VMEM((PR, wide), F32), pltpu.VMEM((NX, PR, wide), F32),
            buf(2, NZ, 16, wide), buf(2, NZ, 16, wide), buf(2, NZ, 16, wide), buf(2, NZ, 16, wide),
            buf(NY, NZ, 16, wide), buf(NY, NZ, 16, wide),
            buf(NY, NZ, 16, wide), buf(NY, NZ, 16, wide), buf(NZ, 16, wide), buf(NZ, 16, wide),
            pltpu.VMEM((16, wide), F32), pltpu.VMEM((NX, 16, wide), F32), pltpu.VMEM((ROWS, wide), F32),
            pltpu.VMEM((OWNERS, 16, KF), F32), pltpu.VMEM((OWNERS, 16, KF), F32),
            buf(KF, wide), buf(KF, wide),
            pltpu.VMEM((8, KF), F32), pltpu.VMEM((NZ, 8, KF), F32),
            pltpu.VMEM((8, KF), F32), pltpu.VMEM((NY, NX, 8, KF), F32),
            pltpu.VMEM((3, SHELLS * 8, KF), F32),
            dma((2,)), dma((REDUCE_SEMS,)), dma((REDUCE_SEMS,)),
        ],
        compiler_params=pltpu.CompilerParams(
            collective_id=1, has_side_effects=True, vmem_limit_bytes=40 << 20
        ),
    )(partial.reshape(NY, NZ, ROWS, 2 * KF), ctf, slice_cells, expand, left)


def solution(mesh):
    placed = (
        P(("half", "cls", "tile"), None, None),
        P("half", "cls", None, None),
        P(("half", "cls", "tile"), None),
        P(("half", "cls", "tile")),
        P(("half", "cls", "tile")),
        P(),
    )
    return jax.shard_map(
        shards,
        mesh=mesh,
        in_specs=placed,
        out_specs=P("half", ("cls", "tile"), None),
        check_vma=False,
    )
```

```python
import functools
import math

import jax
import jax.numpy as jnp
import numpy as np
from jax import lax
from jax.experimental import pallas as pl
from jax.experimental.pallas import tpu as pltpu
from jax.sharding import PartitionSpec as P

PIX = 256
KF = 128
HK = 64
CLS_DEV = 2
BINS = 16
SHELLS = 64
NY, NZ, NX = 4, 8, 4
OWNERS = NY * NZ
ROWS = 144
PR = 80
PA = 48
GROUP = 8

sharpness = 40.0
ctf_scale = 6.0
amp_phase = 0.1

MESH = pl.DeviceIdType.MESH
BF = jnp.bfloat16
F32 = jnp.float32


def dft_tables():
    sample_pos = np.arange(PIX, dtype=np.int32)[:, None]
    freq_pos = np.arange(KF, dtype=np.int32)[None, :] - KF // 2
    angles = (sample_pos * freq_pos % PIX).astype(np.float32) * np.float32(2.0 * math.pi / PIX)
    scaling = np.float32(1.0 / math.sqrt(PIX))
    bf = jnp.bfloat16
    return (np.cos(angles) * scaling).astype(bf), (np.sin(angles) * scaling).astype(bf)


def ctf_table():
    freq = np.arange(KF, dtype=np.int32) - KF // 2
    radius = (freq[:, None] * freq[:, None] + freq[None, :] * freq[None, :]).astype(
        np.float32
    ) / np.float32(HK * HK)
    factor = (ctf_scale * (1.0 + np.arange(BINS) / BINS)).astype(np.float32)
    return -np.sin(factor[:, None, None] * radius[None] + np.float32(amp_phase)).astype(np.float32)


def expand_tables():
    turn = np.zeros((256, 256), np.float32)
    column = np.zeros((256, 256), np.float32)
    middle = np.zeros((256, 256), np.float32)
    for c in range(1, KF):
        turn[c, KF - c] = 1.0
        turn[KF + c, 2 * KF - c] = -1.0
    column[:KF, 0] = 1.0
    column[KF:, KF] = 1.0
    for c in range(HK + 1):
        middle[c, c] = 1.0
        middle[KF + c, KF + c] = 1.0
    for c in range(1, HK):
        middle[c, KF - c] = 1.0
        middle[KF + c, 2 * KF - c] = -1.0
    return np.concatenate([turn, column, middle], 0)


def row_turn():
    turn = np.zeros((HK, HK), np.float32)
    for r in range(1, HK):
        turn[r, HK - r] = 1.0
    return turn


def dot(a, b):
    return jnp.dot(a, b, preferred_element_type=F32)


def pick(chooser, rows):
    high = rows.astype(BF)
    return dot(chooser, high) + dot(chooser, (rows - high.astype(F32)).astype(BF))


def transform(plane, cs, cst):
    section = dot(plane, cs).astype(BF)
    both = dot(cst, section)
    real = both[:KF, :KF] - both[KF:, KF:]
    imag = -(both[KF:, :KF] + both[:KF, KF:])
    return real, imag


def left_over(part):
    low = part[HK:, :]
    row = lax.broadcasted_iota(jnp.int32, (HK, KF), 0)
    col = lax.broadcasted_iota(jnp.int32, (HK, KF), 1)
    line = jnp.sum(jnp.where((col == row + HK) & (row > 0), low[:, 0:1], 0.0), axis=0, keepdims=True)
    first = lax.broadcasted_iota(jnp.int32, (1, KF), 1) <= HK
    return jnp.where(first, low[0:1, :], line)


def lower_masks(rows):
    row = lax.broadcasted_iota(jnp.int32, (rows, 2 * KF), 0) % KF
    col = lax.broadcasted_iota(jnp.int32, (rows, 2 * KF), 1) % KF
    return (row > HK) & (col == row), (row == HK) & (col <= HK)


def here():
    half, cls, tile = lax.axis_index("half"), lax.axis_index("cls"), lax.axis_index("tile")
    y, z = cls // NZ, cls % NZ

    def at(dy=0, dz=0, dx=0):
        return (half, (y + dy) % NY * NZ + (z + dz) % NZ, (tile + dx) % NX)

    return half, y, z, tile, at


def remote(src, dst, send, recv, device):
    return pltpu.make_async_remote_copy(
        src_ref=src, dst_ref=dst, send_sem=send, recv_sem=recv, device_id=device, device_id_type=MESH
    )


def greet(devices):
    barrier = pltpu.get_barrier_semaphore()
    for device in devices:
        pl.semaphore_signal(barrier, inc=1, device_id=device, device_id_type=MESH)


def greeted(devices):
    pl.semaphore_wait(pltpu.get_barrier_semaphore(), len(devices))


GATHER_SEMS = 80


def gather_kernel(
    plane_any, table_any, g_ref, plane_ref, table_ref, own_ref, copy_sem, send_sem, recv_sem
):
    loads = [
        pltpu.make_async_copy(plane_any, plane_ref, copy_sem.at[0]),
        pltpu.make_async_copy(table_any, table_ref, copy_sem.at[1]),
    ]
    for load in loads:
        load.start()
    _, y, z, tile, at = here()
    friends = [at(dz=k) for k in range(1, NZ)] + [at(dy=1), at(dy=-1), at(dx=1), at(dx=-1)]
    greet(friends)
    for load in loads:
        load.wait()
    line = lax.broadcasted_iota(jnp.int32, (16, KF), 0)
    tail_re = jnp.zeros((16, KF), F32)
    tail_im = jnp.zeros((16, KF), F32)
    for k in range(CLS_DEV):
        real, imag = transform(plane_ref[k], table_ref[0:PIX, :], table_ref[PIX : 2 * PIX, :])
        own_ref[k * HK : (k + 1) * HK, 0:KF] = real[:HK].astype(BF)
        own_ref[k * HK : (k + 1) * HK, KF : 2 * KF] = imag[:HK].astype(BF)
        tail_re = jnp.where(line == k, left_over(real), tail_re)
        tail_im = jnp.where(line == k, left_over(imag), tail_im)
    own_ref[128:144, 0:KF] = tail_re.astype(BF)
    own_ref[128:144, KF : 2 * KF] = tail_im.astype(BF)

    sent = []

    def copy(i, view, device):
        ref = g_ref.at[view]
        return remote(ref, ref, send_sem.at[i], recv_sem.at[i], device)

    def push(view, device):
        i = len(sent)
        out = copy(i, view, device)
        out.start()
        sent.append(out)
        return i

    def take(i, view):
        copy(i, view, at(dz=1)).wait_recv()

    def along(dx):
        return pl.ds(pl.multiple_of(PR + 16 * ((tile + dx) % NX), 16), 16)

    whole, front, back = pl.ds(0, PR), pl.ds(0, PA), pl.ds(PA, PR - PA)
    every, low, high = pl.ds(0, NZ), pl.ds(0, NZ // 2), pl.ds(NZ // 2, NZ // 2)
    mine = along(0)
    g_ref[y, z, whole, :] = own_ref[whole, :]
    g_ref[y, z, mine, :] = own_ref[mine, :]
    up, down = at(dz=1), at(dz=-1)
    north, south = at(dy=1), at(dy=-1)
    east, west = at(dx=1), at(dx=-1)
    yw, ye, yo = (y - 1) % NY, (y + 1) % NY, (y + 2) % NY

    greeted(friends)
    r_tags = {j: push((y, z, mine), at(dz=j)) for j in (4, 3, 5, 2, 6, 1, 7)}
    p_up, p_down = push((y, z, whole), up), push((y, z, whole), down)
    waiting, last = [], []

    def cross(zz):
        waiting.append((zz, push((y, zz, whole), north), push((y, zz, whole), south)))

    def settle():
        zz, a, b = waiting.pop(0)
        take(a, (yw, zz, whole))
        fa = push((yw, zz, front), north)
        take(b, (ye, zz, whole))
        fb = push((ye, zz, back), south)
        last.append((zz, fa, fb))

    def spread(yy):
        return yy, push((yy, every, mine), east), push((yy, every, mine), west)

    x_wait, x_last = [], []

    def x_settle():
        yy, p, q = x_wait.pop(0)
        take(p, (yy, every, along(-1)))
        fp = push((yy, low, along(-1)), east)
        take(q, (yy, every, along(1)))
        fq = push((yy, high, along(1)), west)
        x_last.append((yy, fp, fq))

    cross(z)
    for j, tag in r_tags.items():
        take(tag, (y, (z - j) % NZ, mine))
    ra, rb = push((y, every, mine), north), push((y, every, mine), south)
    x_wait.append(spread(y))
    for d in range(1, 5):
        zm, zp = (z - d) % NZ, (z + d) % NZ
        take(p_up, (y, zm, whole if d < 4 else front))
        if d < 4:
            p_up = push((y, zm, whole if d < 3 else front), up)
        take(p_down, (y, zp, whole if d < 4 else back))
        if d < 4:
            p_down = push((y, zp, whole if d < 3 else back), down)
            cross(zm)
        cross(zp)
        if d == 1:
            take(ra, (yw, every, mine))
            fa = push((yw, low, mine), north)
            x_wait.append(spread(yw))
            take(rb, (ye, every, mine))
            fb = push((ye, high, mine), south)
            x_wait.append(spread(ye))
        elif d == 2:
            take(fa, (yo, low, mine))
            take(fb, (yo, high, mine))
            x_wait.append(spread(yo))
        else:
            x_settle()
        settle()
    while waiting or x_wait:
        if waiting:
            settle()
        if x_wait:
            x_settle()
    for zz, fa, fb in last:
        take(fa, (yo, zz, front))
        take(fb, (yo, zz, back))
    for yy, fp, fq in x_last:
        take(fp, (yy, low, along(2)))
        take(fq, (yy, high, along(2)))
    for out in sent:
        out.wait_send()


def image_kernel(
    owner_ref, class_ref, bin_ref, img_ref, refs_ref, ctf_ref, cs_ref, cst_ref, widen_ref,
    combine_ref, expand_ref, turn_ref, out_ref, acc_ref,
):
    step = pl.program_id(0)

    @pl.when(step == 0)
    def _():
        acc_ref[...] = jnp.zeros_like(acc_ref)

    cs, cst = cs_ref[...], cst_ref[...]
    diag, mid = lower_masks(KF)
    diag, mid = diag[HK:], mid[HK:]
    row8 = lax.broadcasted_iota(jnp.int32, (8, 2 * KF), 0)
    col8 = lax.broadcasted_iota(jnp.int32, (8, 2 * KF), 1)

    def halves(section):
        both = dot(cst, section)
        return both[:KF, :KF] - both[KF:, KF:], -(both[KF:, :KF] + both[:KF, KF:])

    section = dot(img_ref[...].reshape(GROUP * PIX, PIX), cs).astype(BF)
    which = [(owner_ref[step * GROUP + g], class_ref[step * GROUP + g], bin_ref[step * GROUP + g]) for g in range(GROUP)]
    tops = [refs_ref[o, pl.ds(pl.multiple_of(k * HK, HK), HK), :] for o, k, _ in which]
    backs = dot(jnp.concatenate(tops, 0), expand_ref[0:256, :]).astype(BF)
    fills = []
    for o, k, _ in which:
        tail = refs_ref[o, 128:144, :].astype(F32)
        extra = jnp.where(k > 0, tail[1:2, :], tail[0:1, :])
        fills.append(jnp.concatenate(
            [jnp.where(diag, extra, 0.0).astype(BF), jnp.where(mid, extra, 0.0).astype(BF)], 1
        ))
    filled = dot(jnp.concatenate(fills, 0), expand_ref[256:768, :])
    loaded, crosses = [], []
    for g in range(GROUP):
        o, k, b = which[g]
        im_re, im_im = halves(section[g * PIX : (g + 1) * PIX])
        im_re, im_im = im_re.astype(BF).astype(F32), im_im.astype(BF).astype(F32)
        low = dot(turn_ref[...], backs[g * HK : (g + 1) * HK]) + filled[g * HK : (g + 1) * HK]
        full = jnp.concatenate([tops[g].astype(F32), low], 0)
        ref_re, ref_im = full[:, :KF], full[:, KF:]
        ctf = ctf_ref[b]
        cross_re = ctf * (ref_re * im_re + ref_im * im_im)
        cross_im = ctf * (ref_re * im_im - ref_im * im_re)
        crosses.append(jnp.concatenate([cross_re, cross_im], 1).astype(BF))
        ref_power = jnp.sum(ctf * ctf * (ref_re * ref_re + ref_im * ref_im), keepdims=True)
        image_power = jnp.sum(im_re * im_re + im_im * im_im, keepdims=True)
        scale = (PIX * sharpness) / jnp.sqrt(ref_power * image_power + 1e-06)
        loaded.append((im_re, im_im, scale))
    inner = dot(jnp.concatenate(crosses, 0), widen_ref[...]).astype(BF)
    posteriors = []
    for g in range(GROUP):
        part = inner[g * KF : (g + 1) * KF]
        stacked = jnp.concatenate([part[:, :PIX], part[:, PIX:]], 0)
        scores = dot(combine_ref[...], stacked)
        weights = jnp.exp(scores * loaded[g][2] - sharpness)
        total = jnp.sum(weights, keepdims=True)
        posteriors.append((weights * (1.0 / total)).astype(BF))
    section = dot(jnp.concatenate(posteriors, 0), cs).astype(BF)
    for g in range(GROUP):
        o, k, b = which[g]
        im_re, im_im, _ = loaded[g]
        sh_re, sh_im = halves(section[g * PIX : (g + 1) * PIX])
        ctf = PIX * ctf_ref[b]
        data_re = ctf * (sh_re * im_re + sh_im * im_im)
        data_im = ctf * (sh_re * im_im - sh_im * im_re)
        rows = pl.ds(pl.multiple_of(k * HK, HK), HK)
        acc_ref[o, rows, 0:KF] += data_re[:HK]
        acc_ref[o, rows, KF : 2 * KF] += data_im[:HK]
        extra = jnp.concatenate([left_over(data_re), left_over(data_im)], 1)
        count = jnp.where((row8 == 2) & (col8 == k * BINS + b), 1.0, 0.0)
        acc_ref[o, 128:136, :] += jnp.where(row8 == k, extra, count)

    @pl.when(step == pl.num_programs(0) - 1)
    def _():
        out_ref[...] = acc_ref[...].astype(BF)


REDUCE_SEMS = 160
Z_ORDER = (4, 3, 5, 2, 6, 1, 7, 0)


def routes(cells, cls, tile):
    cells = cells.astype(F32)
    row = lax.broadcasted_iota(jnp.int32, (OWNERS, 2 * OWNERS), 0)
    col = lax.broadcasted_iota(jnp.int32, (OWNERS, 2 * OWNERS), 1)
    pair = [
        pick(jnp.where(col == 2 * row + k, 1.0, 0.0).astype(BF), cells) for k in range(CLS_DEV)
    ]
    cells = jnp.concatenate(pair, 1).astype(jnp.int32)
    block = lax.shift_right_arithmetic(cells, 7)
    inner = (cells - block * KF + 1).astype(F32)
    first = lax.broadcasted_iota(jnp.int32, (256, 256), 0)
    second = lax.broadcasted_iota(jnp.int32, (256, 256), 1)
    mine = block == cls * NX + tile
    strict = jnp.where(first < second, 1.0, 0.0).astype(BF)
    before = dot(jnp.where(mine, 1.0, 0.0).astype(BF), strict)
    owner = lax.broadcasted_iota(jnp.int32, (OWNERS, OWNERS * 16), 0)
    lane = lax.broadcasted_iota(jnp.int32, (OWNERS, OWNERS * 16), 1)
    here_ = (lax.shift_right_arithmetic(lane, 4) == owner) & ((lane & 15) < 12)
    table = jnp.zeros((OWNERS, OWNERS * 16), F32)
    for r in range(4):
        cell = jnp.sum(jnp.where(mine & (before == r), inner, 0.0), axis=1, keepdims=True)
        table = jnp.where(here_ & ((lane & 3) == r), cell, table)
    cell = (jnp.sum(table, axis=0, keepdims=True) - 1.0).astype(jnp.int32)
    owner = lax.broadcasted_iota(jnp.int32, (OWNERS, 256), 0)
    own = jnp.sum(jnp.where(owner == cls, block.astype(F32), 0.0), axis=0, keepdims=True)
    turned = jnp.sum(jnp.where(first == second, own, 0.0), axis=1, keepdims=True)
    same = jnp.where((turned == own) & (first < second), 1.0, 0.0)
    rank = jnp.sum(same, axis=0, keepdims=True).astype(jnp.int32)
    own = own.astype(jnp.int32)
    slot = lax.shift_right_arithmetic(own, 2) * 16 + rank
    return jnp.where((own & 3) == tile, slot, -4096), cell


def reduce_kernel(
    d_ref, ctf_ref, cells_ref, expand_any, left_any, o_ref,
    expand_ref, left_ref, pin_p, pin_m, ps_p, ps_m, pr_p, pr_m, pz_s, pz_r, px_s, px_r,
    rin_p, rin_m, rs_p, rs_m, rr_p, rr_m, ry_s, ry_r, rz_s, rz_r, rx_s, rx_r,
    held, sb, rb, wz_s, wz_r, sz_s, sz_r, sx_s, sx_r, bins,
    copy_sem, send_sem, recv_sem,
):
    half, y, z, tile, at = here()
    cls = y * NZ + z
    north, south = at(dy=1), at(dy=-1)
    east, west = at(dx=1), at(dx=-1)
    twin = (1 - half, cls, tile)

    def owner_at(k):
        return (half, (cls + k) % OWNERS, tile)

    tables = [
        pltpu.make_async_copy(expand_any, expand_ref, copy_sem.at[0]),
        pltpu.make_async_copy(left_any, left_ref, copy_sem.at[1]),
    ]
    for table in tables:
        table.start()
    plane_peers = {
        (dy, dx): at(dy=dy, dx=dx) for dy in (2, 1, 3, 0) for dx in (2, 1, 3, 0) if dy or dx
    }
    friends = [at(dz=k) for k in range(1, NZ)] + [north, south, at(dy=2), east, west, at(dx=2), twin]
    greet(friends)
    slot, cell = routes(cells_ref[...], cls, tile)
    place = lax.broadcasted_iota(jnp.int32, (OWNERS * 16, 2 * KF), 0)
    chooser = jnp.concatenate(
        [jnp.where(place == slot + 4 * c, 1.0, 0.0).astype(BF) for c in range(3)], 1
    )
    d0 = lax.broadcasted_iota(jnp.int32, (KF, KF), 0) - HK
    d1 = lax.broadcasted_iota(jnp.int32, (KF, KF), 1) - HK
    plane = cls * NX + tile - HK
    radius = plane * plane + d0 * d0 + d1 * d1
    shell = jnp.zeros((KF, KF), jnp.int32)
    for s in range(1, SHELLS):
        shell = jnp.where(radius >= s * s, s, shell)
    greeted(friends)
    sent = []

    def push(src, dst, device):
        i = len(sent)
        out = remote(src, dst, send_sem.at[i], recv_sem.at[i], device)
        out.start()
        sent.append(out)
        return i

    def take(i, dst):
        remote(dst, dst, send_sem.at[i], recv_sem.at[i], east).wait_recv()

    def along(dx):
        return pl.ds(pl.multiple_of(PR + 16 * ((tile + dx) % NX), 16), 16)

    def f(v):
        return v.astype(F32)

    yn, ys, yo = (y + 1) % NY, (y - 1) % NY, (y + 2) % NY
    front, back = pl.ds(0, PA), pl.ds(PA, PR - PA)
    every = pl.ds(0, NZ)
    first_p, first_r = {}, {}
    for n, j in enumerate(Z_ORDER):
        zz = (z + j) % NZ
        if n < NY:
            if n < 2:
                first_r[n] = push(d_ref.at[n, every, along(2)], rin_p.at[n], east)
            else:
                first_r[n] = push(d_ref.at[n, every, along(2)], rin_m.at[n - 2], west)
        first_p[j] = (
            push(d_ref.at[yo, zz, front], pin_p.at[j], north),
            push(d_ref.at[yo, zz, back], pin_m.at[j], south),
        )
    plain_p, plain_r = {}, {}
    for n in range(NY):
        if n < 2:
            plain_r[n] = push(d_ref.at[n, every, along(-1)], rr_m.at[n], west)
        else:
            plain_r[n] = push(d_ref.at[n, every, along(1)], rr_p.at[n], east)

    def plain(j):
        zz = (z + j) % NZ
        plain_p[j] = (
            push(d_ref.at[yn, zz, back], pr_p.at[j, back], north),
            push(d_ref.at[ys, zz, front], pr_m.at[j, front], south),
        )

    second_p, second_r, third_p = {}, {}, {}

    def relay(j):
        zz = (z + j) % NZ
        a, b = first_p[j]
        take(a, pin_p.at[j])
        ps_p[j] = (f(d_ref[yn, zz, front]) + f(pin_p[j])).astype(BF)
        a = push(ps_p.at[j], pr_p.at[j, front], north)
        take(b, pin_m.at[j])
        ps_m[j] = (f(d_ref[ys, zz, back]) + f(pin_m[j])).astype(BF)
        b = push(ps_m.at[j], pr_m.at[j, back], south)
        second_p[j] = a, b

    def relay_r(n):
        if n < 2:
            take(first_r[n], rin_p.at[n])
            rs_p[n] = (f(d_ref[n, every, along(1)]) + f(rin_p[n])).astype(BF)
            second_r[n] = push(rs_p.at[n], rr_p.at[n], east)
        else:
            take(first_r[n], rin_m.at[n - 2])
            rs_m[n - 2] = (f(d_ref[n, every, along(-1)]) + f(rin_m[n - 2])).astype(BF)
            second_r[n] = push(rs_m.at[n - 2], rr_m.at[n], west)

    def settle(j):
        zz = (z + j) % NZ
        a, b = plain_p[j]
        take(a, pr_p.at[j, back])
        take(b, pr_m.at[j, front])
        a, b = second_p[j]
        take(a, pr_p.at[j, front])
        take(b, pr_m.at[j, back])
        pz_s[j] = (f(d_ref[y, zz, pl.ds(0, PR)]) + f(pr_p[j]) + f(pr_m[j])).astype(BF)
        if j:
            third_p[j] = push(pz_s.at[j], pz_r.at[j], at(dz=j))

    def settle_r(n):
        take(second_r[n], (rr_p if n < 2 else rr_m).at[n])
        take(plain_r[n], (rr_m if n < 2 else rr_p).at[n])
        ry_s[n] = (f(d_ref[n, every, along(0)]) + f(rr_p[n]) + f(rr_m[n])).astype(BF)

    for j in Z_ORDER[:3]:
        plain(j)
    for n in range(NZ + 3):
        if n < NZ:
            if n < NY:
                relay_r(n)
            relay(Z_ORDER[n])
            if n + 3 < NZ:
                plain(Z_ORDER[n + 3])
        if n >= 3:
            if n < 3 + NY:
                settle_r(n - 3)
            settle(Z_ORDER[n - 3])
        if n == 2 + NY:
            third_r = {k: push(ry_s.at[(y + k) % NY], ry_r.at[k], at(dy=k)) for k in (2, 1, 3)}
        if n == 4 + NY:
            total = f(ry_s[y])
            for k in (1, 2, 3):
                take(third_r[k], ry_r.at[k])
                total = total + f(ry_r[k])
            rz_s[...] = total.astype(BF)
            fourth_r = {
                j: push(rz_s.at[(z + j) % NZ], rz_r.at[j], at(dz=j)) for j in Z_ORDER[:-1]
            }

    total = f(rz_s[z])
    for j in range(1, NZ):
        take(fourth_r[j], rz_r.at[j])
        total = total + f(rz_r[j])
    rx_s[...] = total
    fifth_r = {k: push(rx_s, rx_r.at[k], at(dx=k)) for k in (2, 1, 3)}
    total = f(pz_s[0])
    for j in range(1, NZ):
        take(third_p[j], pz_r.at[j])
        total = total + f(pz_r[j])
    px_s[...] = total
    fourth_p = {k: push(px_s, px_r.at[k], at(dx=k)) for k in (2, 1, 3)}
    held[along(0), :] = rx_s[...]
    for k in (1, 2, 3):
        take(fifth_r[k], rx_r.at[k])
        held[along(-k), :] = rx_r[k]
    counts = held[128:144]
    weights = []
    for k in range(CLS_DEV):
        weight = jnp.zeros((KF, KF), F32)
        for b in range(BINS):
            ctf = ctf_ref[b]
            weight = weight + counts[2:3, k * BINS + b : k * BINS + b + 1] * (ctf * ctf)
        weights.append(weight)
    for table in tables:
        table.wait()
    total = px_s[...]
    for k in (1, 2, 3):
        take(fourth_p[k], px_r.at[k])
        total = total + px_r[k]
    held[0:PR] = total

    sums = held[...]
    spread = pick(left_ref[...], sums)
    diag, mid = lower_masks(2 * KF)
    extra = spread[512:768]
    parts = jnp.concatenate(
        [spread[256:512], jnp.where(diag, extra, 0.0), jnp.where(mid, extra, 0.0)], 1
    )
    high = parts.astype(BF)
    rest = (parts - f(high)).astype(BF)
    data = spread[0:256] + dot(high, expand_ref[...]) + dot(rest, expand_ref[...])
    packed = pick(chooser, jnp.concatenate([data[:, :KF], data[:, KF:]] + weights, 0))
    sb[...] = packed.reshape(OWNERS, 16, KF)
    rb[cls] = sb[cls]
    used = pl.ds(0, 12)
    went = {
        k: push(sb.at[(cls + k) % OWNERS, used], rb.at[cls, used], owner_at(k)) for k in range(1, OWNERS)
    }
    place = lax.broadcasted_iota(jnp.int32, (KF, OWNERS * 16), 0)
    kind = lax.shift_right_arithmetic(
        lax.broadcasted_iota(jnp.int32, (KF, OWNERS * 16), 1) & 15, 2
    )
    hit = place == cell
    hits = jnp.concatenate(
        [jnp.where(hit & (kind == c), 1.0, 0.0).astype(BF) for c in range(3)], 0
    )
    for k in range(1, OWNERS):
        rb[(cls - k) % OWNERS, 12:16] = jnp.zeros((4, KF), F32)
    for k in range(1, OWNERS):
        take(went[k], rb.at[(cls - k) % OWNERS, used])

    volume = pick(hits, rb[...].reshape(OWNERS * 16, KF))
    scale = 1.0 / (volume[2 * KF :] + 1.0)
    w_re, w_im = volume[:KF] * scale, volume[KF : 2 * KF] * scale
    wz_s[:, 0:KF] = w_re.astype(BF)
    wz_s[:, KF : 2 * KF] = w_im.astype(BF)
    i = push(wz_s, wz_r, twin)
    bins[3 * SHELLS :, :] = jnp.zeros((SHELLS, KF), F32)

    def collect(q, v):
        for s in range(SHELLS):
            part = jnp.sum(jnp.where(shell == s, v, 0.0), axis=0, keepdims=True)
            bins[q * SHELLS + s : q * SHELLS + s + 1, :] = part

    collect(1, w_re * w_re + w_im * w_im)
    take(i, wz_r)
    o_re, o_im = f(wz_r[:, 0:KF]), f(wz_r[:, KF : 2 * KF])
    collect(0, w_re * o_re + w_im * o_im)
    collect(2, o_re * o_re + o_im * o_im)

    def across(v):
        return lax.dot_general(
            jnp.ones((8, KF), BF), v, (((1,), (1,)), ((), ())), preferred_element_type=F32
        )

    rest = bins[...]
    sums = jnp.zeros((8, 4 * SHELLS), F32)
    for _ in range(3):
        high = rest.astype(BF)
        sums = sums + across(high)
        rest = rest - f(high)
    sz_s[...] = sums
    tags = {j: push(sz_s, sz_r.at[j], at(dz=j)) for j in Z_ORDER[:-1]}
    for j, tag in tags.items():
        take(tag, sz_r.at[j])
        sums = sums + sz_r[j]
    sx_s[...] = sums
    tags = {k: push(sx_s, sx_r.at[k[0], k[1]], device) for k, device in plane_peers.items()}
    for k, tag in tags.items():
        take(tag, sx_r.at[k[0], k[1]])
        sums = sums + sx_r[k[0], k[1]]
    sums = [sums[0:1, q * SHELLS : (q + 1) * SHELLS] for q in range(3)]
    fsc = sums[0] / jnp.maximum(jnp.sqrt(sums[1] * sums[2]), 1.0)
    fsc = jnp.maximum(fsc, 0.0)
    gain = jnp.sqrt(2.0 * fsc / (1.0 + fsc))
    voxel = jnp.zeros((KF, KF), F32)
    for s in range(SHELLS):
        voxel = jnp.where(shell == s, gain[:, s : s + 1], voxel)
    o_ref[0, :, 0:KF] = w_re * voxel
    o_ref[0, :, KF : 2 * KF] = w_im * voxel
    for out in sent:
        out.wait_send()


def left_table():
    table = np.zeros((768, ROWS), np.float32)
    for k in range(CLS_DEV):
        for r in range(KF):
            if r < HK:
                table[k * KF + r, k * HK + r] = 1.0
            elif r > HK:
                table[256 + k * KF + r, k * HK + KF - r] = 1.0
            table[512 + k * KF + r, 2 * HK + k] = 1.0
    return table


def shards(images, references, image_owner, image_class, defocus_bin, slice_cells):
    cos_table, sin_table = dft_tables()
    cs = jnp.asarray(np.concatenate([cos_table, sin_table], 1))
    cst = jnp.asarray(np.concatenate([cos_table.T, sin_table.T], 0))
    both = jnp.asarray(
        np.concatenate(
            [np.concatenate([cos_table, sin_table], 1), np.concatenate([cos_table.T, sin_table.T], 0)], 0
        )
    )
    widen = jnp.asarray(
        np.concatenate(
            [
                np.concatenate([cos_table.T, sin_table.T], 1),
                np.concatenate([-sin_table.T, cos_table.T], 1),
            ],
            0,
        )
    )
    combine = jnp.asarray(np.concatenate([cos_table, -sin_table], 1))
    ctf = jnp.asarray(ctf_table())
    expand = jnp.asarray(expand_tables(), BF)
    turn = jnp.asarray(row_turn(), BF)
    left = jnp.asarray(left_table(), BF)
    local = images.shape[0]
    vmem = pl.BlockSpec(memory_space=pltpu.VMEM)
    anywhere = pl.BlockSpec(memory_space=pltpu.HBM)
    dma = pltpu.SemaphoreType.DMA

    spectra = pl.pallas_call(
        gather_kernel,
        name="gather_references",
        out_shape=jax.ShapeDtypeStruct((NY, NZ, ROWS, 2 * KF), BF),
        in_specs=[anywhere] * 2,
        out_specs=vmem,
        scratch_shapes=[
            pltpu.VMEM((CLS_DEV, PIX, PIX), BF), pltpu.VMEM((2 * PIX, 2 * KF), BF),
            pltpu.VMEM((ROWS, 2 * KF), BF), dma((2,)), dma((GATHER_SEMS,)), dma((GATHER_SEMS,)),
        ],
        compiler_params=pltpu.CompilerParams(
            collective_id=0, has_side_effects=True, vmem_limit_bytes=44 << 20
        ),
    )(references[0], both)

    partial = pl.pallas_call(
        image_kernel,
        name="image_terms",
        out_shape=jax.ShapeDtypeStruct((OWNERS, ROWS, 2 * KF), BF),
        grid_spec=pltpu.PrefetchScalarGridSpec(
            num_scalar_prefetch=3,
            grid=(local // GROUP,),
            in_specs=[
                pl.BlockSpec((GROUP, PIX, PIX), lambda i, *_: (i, 0, 0)),
                *[vmem] * 8,
            ],
            out_specs=vmem,
            scratch_shapes=[pltpu.VMEM((OWNERS, ROWS, 2 * KF), F32)],
        ),
        compiler_params=pltpu.CompilerParams(
            dimension_semantics=("arbitrary",), vmem_limit_bytes=44 << 20
        ),
    )(
        image_owner[:, 0], image_class, defocus_bin, images,
        spectra.reshape(OWNERS, ROWS, 2 * KF), ctf, cs, cst, widen, combine, expand, turn,
    )

    def buf(*shape):
        return pltpu.VMEM(shape, BF)

    wide = 2 * KF
    return pl.pallas_call(
        reduce_kernel,
        name="reduce_maps",
        out_shape=jax.ShapeDtypeStruct((1, KF, 2 * KF), F32),
        in_specs=[vmem] * 3 + [anywhere] * 2,
        out_specs=vmem,
        scratch_shapes=[
            buf(768, 256), buf(768, ROWS), buf(NZ, PA, wide), buf(NZ, PR - PA, wide),
            buf(NZ, PA, wide), buf(NZ, PR - PA, wide), buf(NZ, PR, wide), buf(NZ, PR, wide),
            buf(NZ, PR, wide), buf(NZ, PR, wide),
            pltpu.VMEM((PR, wide), F32), pltpu.VMEM((NX, PR, wide), F32),
            buf(2, NZ, 16, wide), buf(2, NZ, 16, wide), buf(2, NZ, 16, wide), buf(2, NZ, 16, wide),
            buf(NY, NZ, 16, wide), buf(NY, NZ, 16, wide),
            buf(NY, NZ, 16, wide), buf(NY, NZ, 16, wide), buf(NZ, 16, wide), buf(NZ, 16, wide),
            pltpu.VMEM((16, wide), F32), pltpu.VMEM((NX, 16, wide), F32), pltpu.VMEM((ROWS, wide), F32),
            pltpu.VMEM((OWNERS, 16, KF), F32), pltpu.VMEM((OWNERS, 16, KF), F32),
            buf(KF, wide), buf(KF, wide),
            pltpu.VMEM((8, 4 * SHELLS), F32), pltpu.VMEM((NZ, 8, 4 * SHELLS), F32),
            pltpu.VMEM((8, 4 * SHELLS), F32), pltpu.VMEM((NY, NX, 8, 4 * SHELLS), F32),
            pltpu.VMEM((4 * SHELLS, KF), F32),
            dma((2,)), dma((REDUCE_SEMS,)), dma((REDUCE_SEMS,)),
        ],
        compiler_params=pltpu.CompilerParams(
            collective_id=1, has_side_effects=True, vmem_limit_bytes=40 << 20
        ),
    )(partial.reshape(NY, NZ, ROWS, 2 * KF), ctf, slice_cells, expand, left)


def solution(mesh):
    placed = (
        P(("half", "cls", "tile"), None, None),
        P("half", "cls", None, None),
        P(("half", "cls", "tile"), None),
        P(("half", "cls", "tile")),
        P(("half", "cls", "tile")),
        P(),
    )
    return jax.shard_map(
        shards,
        mesh=mesh,
        in_specs=placed,
        out_specs=P("half", ("cls", "tile"), None),
        check_vma=False,
    )
```

```python
import functools
import math

import jax
import jax.numpy as jnp
import numpy as np
from jax import lax
from jax.experimental import pallas as pl
from jax.experimental.pallas import tpu as pltpu
from jax.sharding import PartitionSpec as P

PIX = 256
KF = 128
HK = 64
CLS_DEV = 2
BINS = 16
SHELLS = 64
NY, NZ, NX = 4, 8, 4
OWNERS = NY * NZ
ROWS = 144
PR = 80
PA = 48
GROUP = 8

sharpness = 40.0
ctf_scale = 6.0
amp_phase = 0.1

MESH = pl.DeviceIdType.MESH
BF = jnp.bfloat16
F32 = jnp.float32


def dft_tables():
    sample_pos = np.arange(PIX, dtype=np.int32)[:, None]
    freq_pos = np.arange(KF, dtype=np.int32)[None, :] - KF // 2
    angles = (sample_pos * freq_pos % PIX).astype(np.float32) * np.float32(2.0 * math.pi / PIX)
    scaling = np.float32(1.0 / math.sqrt(PIX))
    bf = jnp.bfloat16
    return (np.cos(angles) * scaling).astype(bf), (np.sin(angles) * scaling).astype(bf)


def ctf_table():
    freq = np.arange(KF, dtype=np.int32) - KF // 2
    radius = (freq[:, None] * freq[:, None] + freq[None, :] * freq[None, :]).astype(
        np.float32
    ) / np.float32(HK * HK)
    factor = (ctf_scale * (1.0 + np.arange(BINS) / BINS)).astype(np.float32)
    return -np.sin(factor[:, None, None] * radius[None] + np.float32(amp_phase)).astype(np.float32)


def expand_tables():
    turn = np.zeros((256, 256), np.float32)
    column = np.zeros((256, 256), np.float32)
    middle = np.zeros((256, 256), np.float32)
    for c in range(1, KF):
        turn[c, KF - c] = 1.0
        turn[KF + c, 2 * KF - c] = -1.0
    column[:KF, 0] = 1.0
    column[KF:, KF] = 1.0
    for c in range(HK + 1):
        middle[c, c] = 1.0
        middle[KF + c, KF + c] = 1.0
    for c in range(1, HK):
        middle[c, KF - c] = 1.0
        middle[KF + c, 2 * KF - c] = -1.0
    return np.concatenate([turn, column, middle], 0)


def row_turn():
    turn = np.zeros((HK, HK), np.float32)
    for r in range(1, HK):
        turn[r, HK - r] = 1.0
    return turn


def dot(a, b):
    return jnp.dot(a, b, preferred_element_type=F32)


def pick(chooser, rows):
    high = rows.astype(BF)
    return dot(chooser, high) + dot(chooser, (rows - high.astype(F32)).astype(BF))


def transform(plane, cs, cst):
    section = dot(plane, cs).astype(BF)
    both = dot(cst, section)
    real = both[:KF, :KF] - both[KF:, KF:]
    imag = -(both[KF:, :KF] + both[:KF, KF:])
    return real, imag


def left_over(part):
    low = part[HK:, :]
    row = lax.broadcasted_iota(jnp.int32, (HK, KF), 0)
    col = lax.broadcasted_iota(jnp.int32, (HK, KF), 1)
    line = jnp.sum(jnp.where((col == row + HK) & (row > 0), low[:, 0:1], 0.0), axis=0, keepdims=True)
    first = lax.broadcasted_iota(jnp.int32, (1, KF), 1) <= HK
    return jnp.where(first, low[0:1, :], line)


def lower_masks(rows):
    row = lax.broadcasted_iota(jnp.int32, (rows, 2 * KF), 0) % KF
    col = lax.broadcasted_iota(jnp.int32, (rows, 2 * KF), 1) % KF
    return (row > HK) & (col == row), (row == HK) & (col <= HK)


def here():
    half, cls, tile = lax.axis_index("half"), lax.axis_index("cls"), lax.axis_index("tile")
    y, z = cls // NZ, cls % NZ

    def at(dy=0, dz=0, dx=0):
        return (half, (y + dy) % NY * NZ + (z + dz) % NZ, (tile + dx) % NX)

    return half, y, z, tile, at


def remote(src, dst, send, recv, device):
    return pltpu.make_async_remote_copy(
        src_ref=src, dst_ref=dst, send_sem=send, recv_sem=recv, device_id=device, device_id_type=MESH
    )


def greet(devices):
    barrier = pltpu.get_barrier_semaphore()
    for device in devices:
        pl.semaphore_signal(barrier, inc=1, device_id=device, device_id_type=MESH)


def greeted(devices):
    pl.semaphore_wait(pltpu.get_barrier_semaphore(), len(devices))


GATHER_SEMS = 80


def gather_kernel(
    plane_any, table_any, g_ref, plane_ref, table_ref, own_ref, copy_sem, send_sem, recv_sem
):
    loads = [
        pltpu.make_async_copy(plane_any, plane_ref, copy_sem.at[0]),
        pltpu.make_async_copy(table_any, table_ref, copy_sem.at[1]),
    ]
    for load in loads:
        load.start()
    _, y, z, tile, at = here()
    friends = [at(dz=k) for k in range(1, NZ)] + [at(dy=1), at(dy=-1), at(dx=1), at(dx=-1)]
    greet(friends)
    for load in loads:
        load.wait()
    line = lax.broadcasted_iota(jnp.int32, (16, KF), 0)
    tail_re = jnp.zeros((16, KF), F32)
    tail_im = jnp.zeros((16, KF), F32)
    for k in range(CLS_DEV):
        real, imag = transform(plane_ref[k], table_ref[0:PIX, :], table_ref[PIX : 2 * PIX, :])
        own_ref[k * HK : (k + 1) * HK, 0:KF] = real[:HK].astype(BF)
        own_ref[k * HK : (k + 1) * HK, KF : 2 * KF] = imag[:HK].astype(BF)
        tail_re = jnp.where(line == k, left_over(real), tail_re)
        tail_im = jnp.where(line == k, left_over(imag), tail_im)
    own_ref[128:144, 0:KF] = tail_re.astype(BF)
    own_ref[128:144, KF : 2 * KF] = tail_im.astype(BF)

    sent = []

    def copy(i, view, device):
        ref = g_ref.at[view]
        return remote(ref, ref, send_sem.at[i], recv_sem.at[i], device)

    def push(view, device):
        i = len(sent)
        out = copy(i, view, device)
        out.start()
        sent.append(out)
        return i

    def take(i, view):
        copy(i, view, at(dz=1)).wait_recv()

    def along(dx):
        return pl.ds(pl.multiple_of(PR + 16 * ((tile + dx) % NX), 16), 16)

    whole, front, back = pl.ds(0, PR), pl.ds(0, PA), pl.ds(PA, PR - PA)
    every, low, high = pl.ds(0, NZ), pl.ds(0, NZ // 2), pl.ds(NZ // 2, NZ // 2)
    mine = along(0)
    g_ref[y, z, whole, :] = own_ref[whole, :]
    g_ref[y, z, mine, :] = own_ref[mine, :]
    up, down = at(dz=1), at(dz=-1)
    north, south = at(dy=1), at(dy=-1)
    east, west = at(dx=1), at(dx=-1)
    yw, ye, yo = (y - 1) % NY, (y + 1) % NY, (y + 2) % NY

    greeted(friends)
    r_tags = {j: push((y, z, mine), at(dz=j)) for j in (4, 3, 5, 2, 6, 1, 7)}
    p_up, p_down = push((y, z, whole), up), push((y, z, whole), down)
    waiting, last = [], []

    def cross(zz):
        waiting.append((zz, push((y, zz, whole), north), push((y, zz, whole), south)))

    def settle():
        zz, a, b = waiting.pop(0)
        take(a, (yw, zz, whole))
        fa = push((yw, zz, front), north)
        take(b, (ye, zz, whole))
        fb = push((ye, zz, back), south)
        last.append((zz, fa, fb))

    def spread(yy):
        return yy, push((yy, every, mine), east), push((yy, every, mine), west)

    x_wait, x_last = [], []

    def x_settle():
        yy, p, q = x_wait.pop(0)
        take(p, (yy, every, along(-1)))
        fp = push((yy, low, along(-1)), east)
        take(q, (yy, every, along(1)))
        fq = push((yy, high, along(1)), west)
        x_last.append((yy, fp, fq))

    cross(z)
    for j, tag in r_tags.items():
        take(tag, (y, (z - j) % NZ, mine))
    ra, rb = push((y, every, mine), north), push((y, every, mine), south)
    x_wait.append(spread(y))
    for d in range(1, 5):
        zm, zp = (z - d) % NZ, (z + d) % NZ
        take(p_up, (y, zm, whole if d < 4 else front))
        if d < 4:
            p_up = push((y, zm, whole if d < 3 else front), up)
        take(p_down, (y, zp, whole if d < 4 else back))
        if d < 4:
            p_down = push((y, zp, whole if d < 3 else back), down)
            cross(zm)
        cross(zp)
        if d == 1:
            take(ra, (yw, every, mine))
            fa = push((yw, low, mine), north)
            x_wait.append(spread(yw))
            take(rb, (ye, every, mine))
            fb = push((ye, high, mine), south)
            x_wait.append(spread(ye))
        elif d == 2:
            take(fa, (yo, low, mine))
            take(fb, (yo, high, mine))
            x_wait.append(spread(yo))
        else:
            x_settle()
        settle()
    while waiting or x_wait:
        if waiting:
            settle()
        if x_wait:
            x_settle()
    for zz, fa, fb in last:
        take(fa, (yo, zz, front))
        take(fb, (yo, zz, back))
    for yy, fp, fq in x_last:
        take(fp, (yy, low, along(2)))
        take(fq, (yy, high, along(2)))
    for out in sent:
        out.wait_send()


def image_kernel(
    owner_ref, class_ref, bin_ref, img_ref, refs_ref, ctf_ref, cs_ref, cst_ref, widen_ref,
    combine_ref, expand_ref, turn_ref, out_ref, acc_ref,
):
    step = pl.program_id(0)

    @pl.when(step == 0)
    def _():
        acc_ref[...] = jnp.zeros_like(acc_ref)

    cs, cst = cs_ref[...], cst_ref[...]
    diag, mid = lower_masks(KF)
    diag, mid = diag[HK:], mid[HK:]
    row8 = lax.broadcasted_iota(jnp.int32, (8, 2 * KF), 0)
    col8 = lax.broadcasted_iota(jnp.int32, (8, 2 * KF), 1)

    def halves(section):
        both = dot(cst, section)
        return both[:KF, :KF] - both[KF:, KF:], -(both[KF:, :KF] + both[:KF, KF:])

    section = dot(img_ref[...].reshape(GROUP * PIX, PIX), cs).astype(BF)
    which = [(owner_ref[step * GROUP + g], class_ref[step * GROUP + g], bin_ref[step * GROUP + g]) for g in range(GROUP)]
    tops = [refs_ref[o, pl.ds(pl.multiple_of(k * HK, HK), HK), :] for o, k, _ in which]
    backs = dot(jnp.concatenate(tops, 0), expand_ref[0:256, :]).astype(BF)
    fills = []
    for o, k, _ in which:
        tail = refs_ref[o, 128:144, :].astype(F32)
        extra = jnp.where(k > 0, tail[1:2, :], tail[0:1, :])
        fills.append(jnp.concatenate(
            [jnp.where(diag, extra, 0.0).astype(BF), jnp.where(mid, extra, 0.0).astype(BF)], 1
        ))
    filled = dot(jnp.concatenate(fills, 0), expand_ref[256:768, :])
    loaded, crosses = [], []
    for g in range(GROUP):
        o, k, b = which[g]
        im_re, im_im = halves(section[g * PIX : (g + 1) * PIX])
        im_re, im_im = im_re.astype(BF).astype(F32), im_im.astype(BF).astype(F32)
        low = dot(turn_ref[...], backs[g * HK : (g + 1) * HK]) + filled[g * HK : (g + 1) * HK]
        full = jnp.concatenate([tops[g].astype(F32), low], 0)
        ref_re, ref_im = full[:, :KF], full[:, KF:]
        ctf = ctf_ref[b]
        cross_re = ctf * (ref_re * im_re + ref_im * im_im)
        cross_im = ctf * (ref_re * im_im - ref_im * im_re)
        crosses.append(jnp.concatenate([cross_re, cross_im], 1).astype(BF))
        ref_power = jnp.sum(ctf * ctf * (ref_re * ref_re + ref_im * ref_im), keepdims=True)
        image_power = jnp.sum(im_re * im_re + im_im * im_im, keepdims=True)
        scale = (PIX * sharpness) / jnp.sqrt(ref_power * image_power + 1e-06)
        loaded.append((im_re, im_im, scale))
    inner = dot(jnp.concatenate(crosses, 0), widen_ref[...]).astype(BF)
    posteriors = []
    for g in range(GROUP):
        part = inner[g * KF : (g + 1) * KF]
        stacked = jnp.concatenate([part[:, :PIX], part[:, PIX:]], 0)
        scores = dot(combine_ref[...], stacked)
        weights = jnp.exp(scores * loaded[g][2] - sharpness)
        total = jnp.sum(weights, keepdims=True)
        posteriors.append((weights * (1.0 / total)).astype(BF))
    section = dot(jnp.concatenate(posteriors, 0), cs).astype(BF)
    for g in range(GROUP):
        o, k, b = which[g]
        im_re, im_im, _ = loaded[g]
        sh_re, sh_im = halves(section[g * PIX : (g + 1) * PIX])
        ctf = PIX * ctf_ref[b]
        data_re = ctf * (sh_re * im_re + sh_im * im_im)
        data_im = ctf * (sh_re * im_im - sh_im * im_re)
        rows = pl.ds(pl.multiple_of(k * HK, HK), HK)
        acc_ref[o, rows, 0:KF] += data_re[:HK]
        acc_ref[o, rows, KF : 2 * KF] += data_im[:HK]
        extra = jnp.concatenate([left_over(data_re), left_over(data_im)], 1)
        count = jnp.where((row8 == 2) & (col8 == k * BINS + b), 1.0, 0.0)
        acc_ref[o, 128:136, :] += jnp.where(row8 == k, extra, count)

    @pl.when(step == pl.num_programs(0) - 1)
    def _():
        out_ref[...] = acc_ref[...].astype(BF)


REDUCE_SEMS = 160
Z_ORDER = (4, 3, 5, 2, 6, 1, 7, 0)


def routes(cells, cls, tile):
    cells = cells.astype(F32)
    row = lax.broadcasted_iota(jnp.int32, (OWNERS, 2 * OWNERS), 0)
    col = lax.broadcasted_iota(jnp.int32, (OWNERS, 2 * OWNERS), 1)
    pair = [
        pick(jnp.where(col == 2 * row + k, 1.0, 0.0).astype(BF), cells) for k in range(CLS_DEV)
    ]
    cells = jnp.concatenate(pair, 1).astype(jnp.int32)
    block = lax.shift_right_arithmetic(cells, 7)
    inner = (cells - block * KF + 1).astype(F32)
    first = lax.broadcasted_iota(jnp.int32, (256, 256), 0)
    second = lax.broadcasted_iota(jnp.int32, (256, 256), 1)
    mine = block == cls * NX + tile
    strict = jnp.where(first < second, 1.0, 0.0).astype(BF)
    before = dot(jnp.where(mine, 1.0, 0.0).astype(BF), strict)
    owner = lax.broadcasted_iota(jnp.int32, (OWNERS, OWNERS * 16), 0)
    lane = lax.broadcasted_iota(jnp.int32, (OWNERS, OWNERS * 16), 1)
    here_ = (lax.shift_right_arithmetic(lane, 4) == owner) & ((lane & 15) < 12)
    table = jnp.zeros((OWNERS, OWNERS * 16), F32)
    for r in range(4):
        cell = jnp.sum(jnp.where(mine & (before == r), inner, 0.0), axis=1, keepdims=True)
        table = jnp.where(here_ & ((lane & 3) == r), cell, table)
    cell = (jnp.sum(table, axis=0, keepdims=True) - 1.0).astype(jnp.int32)
    owner = lax.broadcasted_iota(jnp.int32, (OWNERS, 256), 0)
    own = jnp.sum(jnp.where(owner == cls, block.astype(F32), 0.0), axis=0, keepdims=True)
    turned = jnp.sum(jnp.where(first == second, own, 0.0), axis=1, keepdims=True)
    same = jnp.where((turned == own) & (first < second), 1.0, 0.0)
    rank = jnp.sum(same, axis=0, keepdims=True).astype(jnp.int32)
    own = own.astype(jnp.int32)
    slot = lax.shift_right_arithmetic(own, 2) * 16 + rank
    return jnp.where((own & 3) == tile, slot, -4096), cell


def reduce_kernel(
    d_ref, ctf_ref, cells_ref, expand_any, left_any, o_ref,
    expand_ref, left_ref, pin_p, pin_m, ps_p, ps_m, pr_p, pr_m, pz_s, pz_r, px_s, px_r,
    rin_p, rin_m, rs_p, rs_m, rr_p, rr_m, ry_s, ry_r, rz_s, rz_r, rx_s, rx_r,
    held, sb, rb, wz_s, wz_r, sz_s, sz_r, sx_s, sx_r, bins,
    copy_sem, far_send, far_recv, send_sem, recv_sem,
):
    half, y, z, tile, at = here()
    cls = y * NZ + z
    north, south = at(dy=1), at(dy=-1)
    east, west = at(dx=1), at(dx=-1)
    twin = (1 - half, cls, tile)

    def owner_at(k):
        return (half, (cls + k) % OWNERS, tile)

    tables = [
        pltpu.make_async_copy(expand_any, expand_ref, copy_sem.at[0]),
        pltpu.make_async_copy(left_any, left_ref, copy_sem.at[1]),
    ]
    for table in tables:
        table.start()
    plane_peers = {
        (dy, dx): at(dy=dy, dx=dx) for dy in (2, 1, 3, 0) for dx in (2, 1, 3, 0) if dy or dx
    }
    friends = [at(dz=k) for k in range(1, NZ)] + [north, south, at(dy=2), east, west, at(dx=2), twin]
    greet(friends)
    slot, cell = routes(cells_ref[...], cls, tile)
    place = lax.broadcasted_iota(jnp.int32, (OWNERS * 16, 2 * KF), 0)
    chooser = jnp.concatenate(
        [jnp.where(place == slot + 4 * c, 1.0, 0.0).astype(BF) for c in range(3)], 1
    )
    d0 = lax.broadcasted_iota(jnp.int32, (KF, KF), 0) - HK
    d1 = lax.broadcasted_iota(jnp.int32, (KF, KF), 1) - HK
    plane = cls * NX + tile - HK
    radius = plane * plane + d0 * d0 + d1 * d1
    shell = jnp.zeros((KF, KF), jnp.int32)
    shell = lax.fori_loop(1, SHELLS, lambda s, v: jnp.where(radius >= s * s, s, v), shell)
    rb[:, 12:16, :] = jnp.zeros((OWNERS, 4, KF), F32)
    greeted(friends)
    sent = []

    def push(src, dst, device):
        i = len(sent)
        out = remote(src, dst, send_sem.at[i], recv_sem.at[i], device)
        out.start()
        sent.append(out)
        return i

    def take(i, dst):
        remote(dst, dst, send_sem.at[i], recv_sem.at[i], east).wait_recv()

    def along(dx):
        return pl.ds(pl.multiple_of(PR + 16 * ((tile + dx) % NX), 16), 16)

    def f(v):
        return v.astype(F32)

    yn, ys, yo = (y + 1) % NY, (y - 1) % NY, (y + 2) % NY
    front, back = pl.ds(0, PA), pl.ds(PA, PR - PA)
    every = pl.ds(0, NZ)
    first_p, first_r = {}, {}
    for n, j in enumerate(Z_ORDER):
        zz = (z + j) % NZ
        if n < NY:
            if n < 2:
                first_r[n] = push(d_ref.at[n, every, along(2)], rin_p.at[n], east)
            else:
                first_r[n] = push(d_ref.at[n, every, along(2)], rin_m.at[n - 2], west)
        first_p[j] = (
            push(d_ref.at[yo, zz, front], pin_p.at[j], north),
            push(d_ref.at[yo, zz, back], pin_m.at[j], south),
        )
    plain_p, plain_r = {}, {}
    for n in range(NY):
        if n < 2:
            plain_r[n] = push(d_ref.at[n, every, along(-1)], rr_m.at[n], west)
        else:
            plain_r[n] = push(d_ref.at[n, every, along(1)], rr_p.at[n], east)

    def plain(j):
        zz = (z + j) % NZ
        plain_p[j] = (
            push(d_ref.at[yn, zz, back], pr_p.at[j, back], north),
            push(d_ref.at[ys, zz, front], pr_m.at[j, front], south),
        )

    second_p, second_r, third_p = {}, {}, {}

    def relay(j):
        zz = (z + j) % NZ
        a, b = first_p[j]
        take(a, pin_p.at[j])
        ps_p[j] = (f(d_ref[yn, zz, front]) + f(pin_p[j])).astype(BF)
        a = push(ps_p.at[j], pr_p.at[j, front], north)
        take(b, pin_m.at[j])
        ps_m[j] = (f(d_ref[ys, zz, back]) + f(pin_m[j])).astype(BF)
        b = push(ps_m.at[j], pr_m.at[j, back], south)
        second_p[j] = a, b

    def relay_r(n):
        if n < 2:
            take(first_r[n], rin_p.at[n])
            rs_p[n] = (f(d_ref[n, every, along(1)]) + f(rin_p[n])).astype(BF)
            second_r[n] = push(rs_p.at[n], rr_p.at[n], east)
        else:
            take(first_r[n], rin_m.at[n - 2])
            rs_m[n - 2] = (f(d_ref[n, every, along(-1)]) + f(rin_m[n - 2])).astype(BF)
            second_r[n] = push(rs_m.at[n - 2], rr_m.at[n], west)

    def settle(j):
        zz = (z + j) % NZ
        a, b = plain_p[j]
        take(a, pr_p.at[j, back])
        take(b, pr_m.at[j, front])
        a, b = second_p[j]
        take(a, pr_p.at[j, front])
        take(b, pr_m.at[j, back])
        pz_s[j] = (f(d_ref[y, zz, pl.ds(0, PR)]) + f(pr_p[j]) + f(pr_m[j])).astype(BF)
        if j:
            third_p[j] = push(pz_s.at[j], pz_r.at[j], at(dz=j))

    def settle_r(n):
        take(second_r[n], (rr_p if n < 2 else rr_m).at[n])
        take(plain_r[n], (rr_m if n < 2 else rr_p).at[n])
        ry_s[n] = (f(d_ref[n, every, along(0)]) + f(rr_p[n]) + f(rr_m[n])).astype(BF)

    for j in Z_ORDER[:3]:
        plain(j)
    for n in range(NZ + 3):
        if n < NZ:
            if n < NY:
                relay_r(n)
            relay(Z_ORDER[n])
            if n + 3 < NZ:
                plain(Z_ORDER[n + 3])
        if n >= 3:
            if n < 3 + NY:
                settle_r(n - 3)
            settle(Z_ORDER[n - 3])
        if n == 2 + NY:
            third_r = {k: push(ry_s.at[(y + k) % NY], ry_r.at[k], at(dy=k)) for k in (2, 1, 3)}
        if n == 4 + NY:
            total = f(ry_s[y])
            for k in (1, 2, 3):
                take(third_r[k], ry_r.at[k])
                total = total + f(ry_r[k])
            rz_s[...] = total.astype(BF)
            fourth_r = {
                j: push(rz_s.at[(z + j) % NZ], rz_r.at[j], at(dz=j)) for j in Z_ORDER[:-1]
            }

    total = f(rz_s[z])
    for j in range(1, NZ):
        take(fourth_r[j], rz_r.at[j])
        total = total + f(rz_r[j])
    rx_s[...] = total
    fifth_r = {k: push(rx_s, rx_r.at[k], at(dx=k)) for k in (2, 1, 3)}
    total = f(pz_s[0])
    for j in range(1, NZ):
        take(third_p[j], pz_r.at[j])
        total = total + f(pz_r[j])
    px_s[...] = total
    fourth_p = {k: push(px_s, px_r.at[k], at(dx=k)) for k in (2, 1, 3)}
    held[along(0), :] = rx_s[...]
    for k in (1, 2, 3):
        take(fifth_r[k], rx_r.at[k])
        held[along(-k), :] = rx_r[k]
    counts = held[128:144]
    weights = []
    for k in range(CLS_DEV):
        weight = jnp.zeros((KF, KF), F32)
        for b in range(BINS):
            ctf = ctf_ref[b]
            weight = weight + counts[2:3, k * BINS + b : k * BINS + b + 1] * (ctf * ctf)
        weights.append(weight)
    for table in tables:
        table.wait()
    total = px_s[...]
    for k in (1, 2, 3):
        take(fourth_p[k], px_r.at[k])
        total = total + px_r[k]
    held[0:PR] = total

    sums = held[...]
    spread = pick(left_ref[...], sums)
    diag, mid = lower_masks(2 * KF)
    extra = spread[512:768]
    parts = jnp.concatenate(
        [spread[256:512], jnp.where(diag, extra, 0.0), jnp.where(mid, extra, 0.0)], 1
    )
    high = parts.astype(BF)
    rest = (parts - f(high)).astype(BF)
    data = spread[0:256] + dot(high, expand_ref[...]) + dot(rest, expand_ref[...])
    packed = pick(chooser, jnp.concatenate([data[:, :KF], data[:, KF:]] + weights, 0))
    sb[...] = packed.reshape(OWNERS, 16, KF)
    rb[cls] = sb[cls]
    used = pl.ds(0, 12)

    def scatter(k):
        return remote(
            sb.at[(cls + k) % OWNERS, used], rb.at[cls, used], far_send.at[k], far_recv.at[k], owner_at(k)
        )

    def start(k, carry):
        scatter(k).start()
        return carry

    def arrive(k, carry):
        rows = rb.at[(cls + OWNERS - k) % OWNERS, used]
        remote(rows, rows, far_send.at[k], far_recv.at[k], owner_at(k)).wait_recv()
        return carry

    def leave(k, carry):
        scatter(k).wait_send()
        return carry

    lax.fori_loop(1, OWNERS, start, 0)
    place = lax.broadcasted_iota(jnp.int32, (KF, OWNERS * 16), 0)
    kind = lax.shift_right_arithmetic(
        lax.broadcasted_iota(jnp.int32, (KF, OWNERS * 16), 1) & 15, 2
    )
    hit = place == cell
    hits = jnp.concatenate(
        [jnp.where(hit & (kind == c), 1.0, 0.0).astype(BF) for c in range(3)], 0
    )
    lax.fori_loop(1, OWNERS, arrive, 0)

    volume = pick(hits, rb[...].reshape(OWNERS * 16, KF))
    scale = 1.0 / (volume[2 * KF :] + 1.0)
    w_re, w_im = volume[:KF] * scale, volume[KF : 2 * KF] * scale
    wz_s[:, 0:KF] = w_re.astype(BF)
    wz_s[:, KF : 2 * KF] = w_im.astype(BF)
    i = push(wz_s, wz_r, twin)
    bins[3 * SHELLS :, :] = jnp.zeros((SHELLS, KF), F32)

    def collect(parts):
        def some(t, carry):
            for q, v in parts.items():
                lines = [
                    jnp.sum(jnp.where(shell == t * 8 + n, v, 0.0), axis=0, keepdims=True)
                    for n in range(8)
                ]
                bins[pl.ds(pl.multiple_of(q * SHELLS + t * 8, 8), 8), :] = jnp.concatenate(lines, 0)
            return carry

        lax.fori_loop(0, SHELLS // 8, some, 0)

    collect({1: w_re * w_re + w_im * w_im})
    take(i, wz_r)
    o_re, o_im = f(wz_r[:, 0:KF]), f(wz_r[:, KF : 2 * KF])
    collect({0: w_re * o_re + w_im * o_im, 2: o_re * o_re + o_im * o_im})

    def across(v):
        return lax.dot_general(
            jnp.ones((8, KF), BF), v, (((1,), (1,)), ((), ())), preferred_element_type=F32
        )

    rest = bins[...]
    sums = jnp.zeros((8, 4 * SHELLS), F32)
    for _ in range(3):
        high = rest.astype(BF)
        sums = sums + across(high)
        rest = rest - f(high)
    sz_s[...] = sums
    tags = {j: push(sz_s, sz_r.at[j], at(dz=j)) for j in Z_ORDER[:-1]}
    for j, tag in tags.items():
        take(tag, sz_r.at[j])
        sums = sums + sz_r[j]
    sx_s[...] = sums
    tags = {k: push(sx_s, sx_r.at[k[0], k[1]], device) for k, device in plane_peers.items()}
    for k, tag in tags.items():
        take(tag, sx_r.at[k[0], k[1]])
        sums = sums + sx_r[k[0], k[1]]
    sums = [sums[0:1, q * SHELLS : (q + 1) * SHELLS] for q in range(3)]
    fsc = sums[0] / jnp.maximum(jnp.sqrt(sums[1] * sums[2]), 1.0)
    fsc = jnp.maximum(fsc, 0.0)
    gain = jnp.sqrt(2.0 * fsc / (1.0 + fsc))
    voxel = jnp.zeros((KF, KF), F32)
    for s in range(SHELLS):
        voxel = jnp.where(shell == s, gain[:, s : s + 1], voxel)
    o_ref[0, :, 0:KF] = w_re * voxel
    o_ref[0, :, KF : 2 * KF] = w_im * voxel
    lax.fori_loop(1, OWNERS, leave, 0)
    for out in sent:
        out.wait_send()


def left_table():
    table = np.zeros((768, ROWS), np.float32)
    for k in range(CLS_DEV):
        for r in range(KF):
            if r < HK:
                table[k * KF + r, k * HK + r] = 1.0
            elif r > HK:
                table[256 + k * KF + r, k * HK + KF - r] = 1.0
            table[512 + k * KF + r, 2 * HK + k] = 1.0
    return table


def shards(images, references, image_owner, image_class, defocus_bin, slice_cells):
    cos_table, sin_table = dft_tables()
    cs = jnp.asarray(np.concatenate([cos_table, sin_table], 1))
    cst = jnp.asarray(np.concatenate([cos_table.T, sin_table.T], 0))
    both = jnp.asarray(
        np.concatenate(
            [np.concatenate([cos_table, sin_table], 1), np.concatenate([cos_table.T, sin_table.T], 0)], 0
        )
    )
    widen = jnp.asarray(
        np.concatenate(
            [
                np.concatenate([cos_table.T, sin_table.T], 1),
                np.concatenate([-sin_table.T, cos_table.T], 1),
            ],
            0,
        )
    )
    combine = jnp.asarray(np.concatenate([cos_table, -sin_table], 1))
    ctf = jnp.asarray(ctf_table())
    expand = jnp.asarray(expand_tables(), BF)
    turn = jnp.asarray(row_turn(), BF)
    left = jnp.asarray(left_table(), BF)
    local = images.shape[0]
    vmem = pl.BlockSpec(memory_space=pltpu.VMEM)
    anywhere = pl.BlockSpec(memory_space=pltpu.HBM)
    dma = pltpu.SemaphoreType.DMA

    spectra = pl.pallas_call(
        gather_kernel,
        name="gather_references",
        out_shape=jax.ShapeDtypeStruct((NY, NZ, ROWS, 2 * KF), BF),
        in_specs=[anywhere] * 2,
        out_specs=vmem,
        scratch_shapes=[
            pltpu.VMEM((CLS_DEV, PIX, PIX), BF), pltpu.VMEM((2 * PIX, 2 * KF), BF),
            pltpu.VMEM((ROWS, 2 * KF), BF), dma((2,)), dma((GATHER_SEMS,)), dma((GATHER_SEMS,)),
        ],
        compiler_params=pltpu.CompilerParams(
            collective_id=0, has_side_effects=True, vmem_limit_bytes=44 << 20
        ),
    )(references[0], both)

    partial = pl.pallas_call(
        image_kernel,
        name="image_terms",
        out_shape=jax.ShapeDtypeStruct((OWNERS, ROWS, 2 * KF), BF),
        grid_spec=pltpu.PrefetchScalarGridSpec(
            num_scalar_prefetch=3,
            grid=(local // GROUP,),
            in_specs=[
                pl.BlockSpec((GROUP, PIX, PIX), lambda i, *_: (i, 0, 0)),
                *[vmem] * 8,
            ],
            out_specs=vmem,
            scratch_shapes=[pltpu.VMEM((OWNERS, ROWS, 2 * KF), F32)],
        ),
        compiler_params=pltpu.CompilerParams(
            dimension_semantics=("arbitrary",), vmem_limit_bytes=44 << 20
        ),
    )(
        image_owner[:, 0], image_class, defocus_bin, images,
        spectra.reshape(OWNERS, ROWS, 2 * KF), ctf, cs, cst, widen, combine, expand, turn,
    )

    def buf(*shape):
        return pltpu.VMEM(shape, BF)

    wide = 2 * KF
    return pl.pallas_call(
        reduce_kernel,
        name="reduce_maps",
        out_shape=jax.ShapeDtypeStruct((1, KF, 2 * KF), F32),
        in_specs=[vmem] * 3 + [anywhere] * 2,
        out_specs=vmem,
        scratch_shapes=[
            buf(768, 256), buf(768, ROWS), buf(NZ, PA, wide), buf(NZ, PR - PA, wide),
            buf(NZ, PA, wide), buf(NZ, PR - PA, wide), buf(NZ, PR, wide), buf(NZ, PR, wide),
            buf(NZ, PR, wide), buf(NZ, PR, wide),
            pltpu.VMEM((PR, wide), F32), pltpu.VMEM((NX, PR, wide), F32),
            buf(2, NZ, 16, wide), buf(2, NZ, 16, wide), buf(2, NZ, 16, wide), buf(2, NZ, 16, wide),
            buf(NY, NZ, 16, wide), buf(NY, NZ, 16, wide),
            buf(NY, NZ, 16, wide), buf(NY, NZ, 16, wide), buf(NZ, 16, wide), buf(NZ, 16, wide),
            pltpu.VMEM((16, wide), F32), pltpu.VMEM((NX, 16, wide), F32), pltpu.VMEM((ROWS, wide), F32),
            pltpu.VMEM((OWNERS, 16, KF), F32), pltpu.VMEM((OWNERS, 16, KF), F32),
            buf(KF, wide), buf(KF, wide),
            pltpu.VMEM((8, 4 * SHELLS), F32), pltpu.VMEM((NZ, 8, 4 * SHELLS), F32),
            pltpu.VMEM((8, 4 * SHELLS), F32), pltpu.VMEM((NY, NX, 8, 4 * SHELLS), F32),
            pltpu.VMEM((4 * SHELLS, KF), F32),
            dma((2,)), dma((OWNERS,)), dma((OWNERS,)), dma((REDUCE_SEMS,)), dma((REDUCE_SEMS,)),
        ],
        compiler_params=pltpu.CompilerParams(
            collective_id=1, has_side_effects=True, vmem_limit_bytes=40 << 20
        ),
    )(partial.reshape(NY, NZ, ROWS, 2 * KF), ctf, slice_cells, expand, left)


def solution(mesh):
    placed = (
        P(("half", "cls", "tile"), None, None),
        P("half", "cls", None, None),
        P(("half", "cls", "tile"), None),
        P(("half", "cls", "tile")),
        P(("half", "cls", "tile")),
        P(),
    )
    return jax.shard_map(
        shards,
        mesh=mesh,
        in_specs=placed,
        out_specs=P("half", ("cls", "tile"), None),
        check_vma=False,
    )
```

```python
import functools
import math

import jax
import jax.numpy as jnp
import numpy as np
from jax import lax
from jax.experimental import pallas as pl
from jax.experimental.pallas import tpu as pltpu
from jax.sharding import PartitionSpec as P

PIX = 256
KF = 128
HK = 64
CLS_DEV = 2
BINS = 16
SHELLS = 64
NY, NZ, NX = 4, 8, 4
OWNERS = NY * NZ
ROWS = 144
PR = 80
PA = 48
GROUP = 16

sharpness = 40.0
ctf_scale = 6.0
amp_phase = 0.1

MESH = pl.DeviceIdType.MESH
BF = jnp.bfloat16
F32 = jnp.float32


def dft_tables():
    sample_pos = np.arange(PIX, dtype=np.int32)[:, None]
    freq_pos = np.arange(KF, dtype=np.int32)[None, :] - KF // 2
    angles = (sample_pos * freq_pos % PIX).astype(np.float32) * np.float32(2.0 * math.pi / PIX)
    scaling = np.float32(1.0 / math.sqrt(PIX))
    bf = jnp.bfloat16
    return (np.cos(angles) * scaling).astype(bf), (np.sin(angles) * scaling).astype(bf)


def ctf_table():
    freq = np.arange(KF, dtype=np.int32) - KF // 2
    radius = (freq[:, None] * freq[:, None] + freq[None, :] * freq[None, :]).astype(
        np.float32
    ) / np.float32(HK * HK)
    factor = (ctf_scale * (1.0 + np.arange(BINS) / BINS)).astype(np.float32)
    return -np.sin(factor[:, None, None] * radius[None] + np.float32(amp_phase)).astype(np.float32)


def expand_tables():
    turn = np.zeros((256, 256), np.float32)
    column = np.zeros((256, 256), np.float32)
    middle = np.zeros((256, 256), np.float32)
    for c in range(1, KF):
        turn[c, KF - c] = 1.0
        turn[KF + c, 2 * KF - c] = -1.0
    column[:KF, 0] = 1.0
    column[KF:, KF] = 1.0
    for c in range(HK + 1):
        middle[c, c] = 1.0
        middle[KF + c, KF + c] = 1.0
    for c in range(1, HK):
        middle[c, KF - c] = 1.0
        middle[KF + c, 2 * KF - c] = -1.0
    return np.concatenate([turn, column, middle], 0)


def row_turn():
    turn = np.zeros((HK, HK), np.float32)
    for r in range(1, HK):
        turn[r, HK - r] = 1.0
    return turn


def dot(a, b):
    return jnp.dot(a, b, preferred_element_type=F32)


def pick(chooser, rows):
    high = rows.astype(BF)
    return dot(chooser, high) + dot(chooser, (rows - high.astype(F32)).astype(BF))


def transform(plane, cs, cst):
    section = dot(plane, cs).astype(BF)
    both = dot(cst, section)
    real = both[:KF, :KF] - both[KF:, KF:]
    imag = -(both[KF:, :KF] + both[:KF, KF:])
    return real, imag


def left_over(part):
    low = part[HK:, :]
    row = lax.broadcasted_iota(jnp.int32, (HK, KF), 0)
    col = lax.broadcasted_iota(jnp.int32, (HK, KF), 1)
    line = jnp.sum(jnp.where((col == row + HK) & (row > 0), low[:, 0:1], 0.0), axis=0, keepdims=True)
    first = lax.broadcasted_iota(jnp.int32, (1, KF), 1) <= HK
    return jnp.where(first, low[0:1, :], line)


def lower_masks(rows):
    row = lax.broadcasted_iota(jnp.int32, (rows, 2 * KF), 0) % KF
    col = lax.broadcasted_iota(jnp.int32, (rows, 2 * KF), 1) % KF
    return (row > HK) & (col == row), (row == HK) & (col <= HK)


def here():
    half, cls, tile = lax.axis_index("half"), lax.axis_index("cls"), lax.axis_index("tile")
    y, z = cls // NZ, cls % NZ

    def at(dy=0, dz=0, dx=0):
        return (half, (y + dy) % NY * NZ + (z + dz) % NZ, (tile + dx) % NX)

    return half, y, z, tile, at


def remote(src, dst, send, recv, device):
    return pltpu.make_async_remote_copy(
        src_ref=src, dst_ref=dst, send_sem=send, recv_sem=recv, device_id=device, device_id_type=MESH
    )


def greet(devices):
    barrier = pltpu.get_barrier_semaphore()
    for device in devices:
        pl.semaphore_signal(barrier, inc=1, device_id=device, device_id_type=MESH)


def greeted(devices):
    pl.semaphore_wait(pltpu.get_barrier_semaphore(), len(devices))


GATHER_SEMS = 80


def gather_kernel(
    plane_any, table_any, g_ref, plane_ref, table_ref, own_ref, copy_sem, send_sem, recv_sem
):
    loads = [
        pltpu.make_async_copy(plane_any, plane_ref, copy_sem.at[0]),
        pltpu.make_async_copy(table_any, table_ref, copy_sem.at[1]),
    ]
    for load in loads:
        load.start()
    _, y, z, tile, at = here()
    friends = [at(dz=k) for k in range(1, NZ)] + [at(dy=1), at(dy=-1), at(dx=1), at(dx=-1)]
    greet(friends)
    for load in loads:
        load.wait()
    line = lax.broadcasted_iota(jnp.int32, (16, KF), 0)
    tail_re = jnp.zeros((16, KF), F32)
    tail_im = jnp.zeros((16, KF), F32)
    for k in range(CLS_DEV):
        real, imag = transform(plane_ref[k], table_ref[0:PIX, :], table_ref[PIX : 2 * PIX, :])
        own_ref[k * HK : (k + 1) * HK, 0:KF] = real[:HK].astype(BF)
        own_ref[k * HK : (k + 1) * HK, KF : 2 * KF] = imag[:HK].astype(BF)
        tail_re = jnp.where(line == k, left_over(real), tail_re)
        tail_im = jnp.where(line == k, left_over(imag), tail_im)
    own_ref[128:144, 0:KF] = tail_re.astype(BF)
    own_ref[128:144, KF : 2 * KF] = tail_im.astype(BF)

    sent = []

    def copy(i, view, device):
        ref = g_ref.at[view]
        return remote(ref, ref, send_sem.at[i], recv_sem.at[i], device)

    def push(view, device):
        i = len(sent)
        out = copy(i, view, device)
        out.start()
        sent.append(out)
        return i

    def take(i, view):
        copy(i, view, at(dz=1)).wait_recv()

    def along(dx):
        return pl.ds(pl.multiple_of(PR + 16 * ((tile + dx) % NX), 16), 16)

    whole, front, back = pl.ds(0, PR), pl.ds(0, PA), pl.ds(PA, PR - PA)
    every, low, high = pl.ds(0, NZ), pl.ds(0, NZ // 2), pl.ds(NZ // 2, NZ // 2)
    mine = along(0)
    g_ref[y, z, whole, :] = own_ref[whole, :]
    g_ref[y, z, mine, :] = own_ref[mine, :]
    up, down = at(dz=1), at(dz=-1)
    north, south = at(dy=1), at(dy=-1)
    east, west = at(dx=1), at(dx=-1)
    yw, ye, yo = (y - 1) % NY, (y + 1) % NY, (y + 2) % NY

    greeted(friends)
    r_tags = {j: push((y, z, mine), at(dz=j)) for j in (4, 3, 5, 2, 6, 1, 7)}
    p_up, p_down = push((y, z, whole), up), push((y, z, whole), down)
    waiting, last = [], []

    def cross(zz):
        waiting.append((zz, push((y, zz, whole), north), push((y, zz, whole), south)))

    def settle():
        zz, a, b = waiting.pop(0)
        take(a, (yw, zz, whole))
        fa = push((yw, zz, front), north)
        take(b, (ye, zz, whole))
        fb = push((ye, zz, back), south)
        last.append((zz, fa, fb))

    def spread(yy):
        return yy, push((yy, every, mine), east), push((yy, every, mine), west)

    x_wait, x_last = [], []

    def x_settle():
        yy, p, q = x_wait.pop(0)
        take(p, (yy, every, along(-1)))
        fp = push((yy, low, along(-1)), east)
        take(q, (yy, every, along(1)))
        fq = push((yy, high, along(1)), west)
        x_last.append((yy, fp, fq))

    cross(z)
    for j, tag in r_tags.items():
        take(tag, (y, (z - j) % NZ, mine))
    ra, rb = push((y, every, mine), north), push((y, every, mine), south)
    x_wait.append(spread(y))
    for d in range(1, 5):
        zm, zp = (z - d) % NZ, (z + d) % NZ
        take(p_up, (y, zm, whole if d < 4 else front))
        if d < 4:
            p_up = push((y, zm, whole if d < 3 else front), up)
        take(p_down, (y, zp, whole if d < 4 else back))
        if d < 4:
            p_down = push((y, zp, whole if d < 3 else back), down)
            cross(zm)
        cross(zp)
        if d == 1:
            take(ra, (yw, every, mine))
            fa = push((yw, low, mine), north)
            x_wait.append(spread(yw))
            take(rb, (ye, every, mine))
            fb = push((ye, high, mine), south)
            x_wait.append(spread(ye))
        elif d == 2:
            take(fa, (yo, low, mine))
            take(fb, (yo, high, mine))
            x_wait.append(spread(yo))
        else:
            x_settle()
        settle()
    while waiting or x_wait:
        if waiting:
            settle()
        if x_wait:
            x_settle()
    for zz, fa, fb in last:
        take(fa, (yo, zz, front))
        take(fb, (yo, zz, back))
    for yy, fp, fq in x_last:
        take(fp, (yy, low, along(2)))
        take(fq, (yy, high, along(2)))
    for out in sent:
        out.wait_send()


def image_kernel(
    owner_ref, class_ref, bin_ref, img_ref, refs_ref, ctf_ref, cs_ref, cst_ref, widen_ref,
    combine_ref, expand_ref, turn_ref, out_ref, acc_ref,
):
    step = pl.program_id(0)

    @pl.when(step == 0)
    def _():
        acc_ref[...] = jnp.zeros_like(acc_ref)

    cs, cst = cs_ref[...], cst_ref[...]
    diag, mid = lower_masks(KF)
    diag, mid = diag[HK:], mid[HK:]
    row8 = lax.broadcasted_iota(jnp.int32, (8, 2 * KF), 0)
    col8 = lax.broadcasted_iota(jnp.int32, (8, 2 * KF), 1)

    def halves(section):
        both = dot(cst, section)
        return both[:KF, :KF] - both[KF:, KF:], -(both[KF:, :KF] + both[:KF, KF:])

    section = dot(img_ref[...].reshape(GROUP * PIX, PIX), cs).astype(BF)
    which = [(owner_ref[step * GROUP + g], class_ref[step * GROUP + g], bin_ref[step * GROUP + g]) for g in range(GROUP)]
    tops = [refs_ref[o, pl.ds(pl.multiple_of(k * HK, HK), HK), :] for o, k, _ in which]
    backs = dot(jnp.concatenate(tops, 0), expand_ref[0:256, :]).astype(BF)
    fills = []
    for o, k, _ in which:
        tail = refs_ref[o, 128:144, :].astype(F32)
        extra = jnp.where(k > 0, tail[1:2, :], tail[0:1, :])
        fills.append(jnp.concatenate(
            [jnp.where(diag, extra, 0.0).astype(BF), jnp.where(mid, extra, 0.0).astype(BF)], 1
        ))
    filled = dot(jnp.concatenate(fills, 0), expand_ref[256:768, :])
    loaded, crosses = [], []
    for g in range(GROUP):
        o, k, b = which[g]
        im_re, im_im = halves(section[g * PIX : (g + 1) * PIX])
        im_re, im_im = im_re.astype(BF).astype(F32), im_im.astype(BF).astype(F32)
        low = dot(turn_ref[...], backs[g * HK : (g + 1) * HK]) + filled[g * HK : (g + 1) * HK]
        full = jnp.concatenate([tops[g].astype(F32), low], 0)
        ref_re, ref_im = full[:, :KF], full[:, KF:]
        ctf = ctf_ref[b]
        cross_re = ctf * (ref_re * im_re + ref_im * im_im)
        cross_im = ctf * (ref_re * im_im - ref_im * im_re)
        crosses.append(jnp.concatenate([cross_re, cross_im], 1).astype(BF))
        ref_power = jnp.sum(ctf * ctf * (ref_re * ref_re + ref_im * ref_im), keepdims=True)
        image_power = jnp.sum(im_re * im_re + im_im * im_im, keepdims=True)
        scale = (PIX * sharpness) / jnp.sqrt(ref_power * image_power + 1e-06)
        loaded.append((im_re, im_im, scale))
    inner = dot(jnp.concatenate(crosses, 0), widen_ref[...]).astype(BF)
    posteriors = []
    for g in range(GROUP):
        part = inner[g * KF : (g + 1) * KF]
        stacked = jnp.concatenate([part[:, :PIX], part[:, PIX:]], 0)
        scores = dot(combine_ref[...], stacked)
        weights = jnp.exp(scores * loaded[g][2] - sharpness)
        total = jnp.sum(weights, keepdims=True)
        posteriors.append((weights * (1.0 / total)).astype(BF))
    section = dot(jnp.concatenate(posteriors, 0), cs).astype(BF)
    for g in range(GROUP):
        o, k, b = which[g]
        im_re, im_im, _ = loaded[g]
        sh_re, sh_im = halves(section[g * PIX : (g + 1) * PIX])
        ctf = PIX * ctf_ref[b]
        data_re = ctf * (sh_re * im_re + sh_im * im_im)
        data_im = ctf * (sh_re * im_im - sh_im * im_re)
        rows = pl.ds(pl.multiple_of(k * HK, HK), HK)
        acc_ref[o, rows, 0:KF] += data_re[:HK]
        acc_ref[o, rows, KF : 2 * KF] += data_im[:HK]
        extra = jnp.concatenate([left_over(data_re), left_over(data_im)], 1)
        count = jnp.where((row8 == 2) & (col8 == k * BINS + b), 1.0, 0.0)
        acc_ref[o, 128:136, :] += jnp.where(row8 == k, extra, count)

    @pl.when(step == pl.num_programs(0) - 1)
    def _():
        out_ref[...] = acc_ref[...].astype(BF)


REDUCE_SEMS = 160
Z_ORDER = (4, 3, 5, 2, 6, 1, 7, 0)


def routes(cells, cls, tile):
    cells = cells.astype(F32)
    row = lax.broadcasted_iota(jnp.int32, (OWNERS, 2 * OWNERS), 0)
    col = lax.broadcasted_iota(jnp.int32, (OWNERS, 2 * OWNERS), 1)
    pair = [
        pick(jnp.where(col == 2 * row + k, 1.0, 0.0).astype(BF), cells) for k in range(CLS_DEV)
    ]
    cells = jnp.concatenate(pair, 1).astype(jnp.int32)
    block = lax.shift_right_arithmetic(cells, 7)
    inner = (cells - block * KF + 1).astype(F32)
    first = lax.broadcasted_iota(jnp.int32, (256, 256), 0)
    second = lax.broadcasted_iota(jnp.int32, (256, 256), 1)
    mine = block == cls * NX + tile
    strict = jnp.where(first < second, 1.0, 0.0).astype(BF)
    before = dot(jnp.where(mine, 1.0, 0.0).astype(BF), strict)
    owner = lax.broadcasted_iota(jnp.int32, (OWNERS, OWNERS * 16), 0)
    lane = lax.broadcasted_iota(jnp.int32, (OWNERS, OWNERS * 16), 1)
    here_ = (lax.shift_right_arithmetic(lane, 4) == owner) & ((lane & 15) < 12)
    table = jnp.zeros((OWNERS, OWNERS * 16), F32)
    for r in range(4):
        cell = jnp.sum(jnp.where(mine & (before == r), inner, 0.0), axis=1, keepdims=True)
        table = jnp.where(here_ & ((lane & 3) == r), cell, table)
    cell = (jnp.sum(table, axis=0, keepdims=True) - 1.0).astype(jnp.int32)
    owner = lax.broadcasted_iota(jnp.int32, (OWNERS, 256), 0)
    own = jnp.sum(jnp.where(owner == cls, block.astype(F32), 0.0), axis=0, keepdims=True)
    turned = jnp.sum(jnp.where(first == second, own, 0.0), axis=1, keepdims=True)
    same = jnp.where((turned == own) & (first < second), 1.0, 0.0)
    rank = jnp.sum(same, axis=0, keepdims=True).astype(jnp.int32)
    own = own.astype(jnp.int32)
    slot = lax.shift_right_arithmetic(own, 2) * 16 + rank
    return jnp.where((own & 3) == tile, slot, -4096), cell


def reduce_kernel(
    d_ref, ctf_ref, cells_ref, expand_any, left_any, o_ref,
    expand_ref, left_ref, pin_p, pin_m, ps_p, ps_m, pr_p, pr_m, pz_s, pz_r, px_s, px_r,
    rin_p, rin_m, rs_p, rs_m, rr_p, rr_m, ry_s, ry_r, rz_s, rz_r, rx_s, rx_r,
    held, sb, rb, wz_s, wz_r, sz_s, sz_r, sx_s, sx_r, bins,
    copy_sem, send_sem, recv_sem,
):
    half, y, z, tile, at = here()
    cls = y * NZ + z
    north, south = at(dy=1), at(dy=-1)
    east, west = at(dx=1), at(dx=-1)
    twin = (1 - half, cls, tile)

    def owner_at(k):
        return (half, (cls + k) % OWNERS, tile)

    tables = [
        pltpu.make_async_copy(expand_any, expand_ref, copy_sem.at[0]),
        pltpu.make_async_copy(left_any, left_ref, copy_sem.at[1]),
    ]
    for table in tables:
        table.start()
    plane_peers = {
        (dy, dx): at(dy=dy, dx=dx) for dy in (2, 1, 3, 0) for dx in (2, 1, 3, 0) if dy or dx
    }
    friends = [at(dz=k) for k in range(1, NZ)] + [north, south, at(dy=2), east, west, at(dx=2), twin]
    greet(friends)
    slot, cell = routes(cells_ref[...], cls, tile)
    place = lax.broadcasted_iota(jnp.int32, (OWNERS * 16, 2 * KF), 0)
    chooser = jnp.concatenate(
        [jnp.where(place == slot + 4 * c, 1.0, 0.0).astype(BF) for c in range(3)], 1
    )
    d0 = lax.broadcasted_iota(jnp.int32, (KF, KF), 0) - HK
    d1 = lax.broadcasted_iota(jnp.int32, (KF, KF), 1) - HK
    plane = cls * NX + tile - HK
    radius = plane * plane + d0 * d0 + d1 * d1
    shell = jnp.zeros((KF, KF), jnp.int32)
    for s in range(1, SHELLS):
        shell = jnp.where(radius >= s * s, s, shell)
    greeted(friends)
    sent = []

    def push(src, dst, device):
        i = len(sent)
        out = remote(src, dst, send_sem.at[i], recv_sem.at[i], device)
        out.start()
        sent.append(out)
        return i

    def take(i, dst):
        remote(dst, dst, send_sem.at[i], recv_sem.at[i], east).wait_recv()

    def along(dx):
        return pl.ds(pl.multiple_of(PR + 16 * ((tile + dx) % NX), 16), 16)

    def f(v):
        return v.astype(F32)

    yn, ys, yo = (y + 1) % NY, (y - 1) % NY, (y + 2) % NY
    front, back = pl.ds(0, PA), pl.ds(PA, PR - PA)
    every = pl.ds(0, NZ)
    first_p, first_r = {}, {}
    for n, j in enumerate(Z_ORDER):
        zz = (z + j) % NZ
        if n < NY:
            if n < 2:
                first_r[n] = push(d_ref.at[n, every, along(2)], rin_p.at[n], east)
            else:
                first_r[n] = push(d_ref.at[n, every, along(2)], rin_m.at[n - 2], west)
        first_p[j] = (
            push(d_ref.at[yo, zz, front], pin_p.at[j], north),
            push(d_ref.at[yo, zz, back], pin_m.at[j], south),
        )
    plain_p, plain_r = {}, {}
    for n in range(NY):
        if n < 2:
            plain_r[n] = push(d_ref.at[n, every, along(-1)], rr_m.at[n], west)
        else:
            plain_r[n] = push(d_ref.at[n, every, along(1)], rr_p.at[n], east)

    def plain(j):
        zz = (z + j) % NZ
        plain_p[j] = (
            push(d_ref.at[yn, zz, back], pr_p.at[j, back], north),
            push(d_ref.at[ys, zz, front], pr_m.at[j, front], south),
        )

    second_p, second_r, third_p = {}, {}, {}

    def relay(j):
        zz = (z + j) % NZ
        a, b = first_p[j]
        take(a, pin_p.at[j])
        ps_p[j] = (f(d_ref[yn, zz, front]) + f(pin_p[j])).astype(BF)
        a = push(ps_p.at[j], pr_p.at[j, front], north)
        take(b, pin_m.at[j])
        ps_m[j] = (f(d_ref[ys, zz, back]) + f(pin_m[j])).astype(BF)
        b = push(ps_m.at[j], pr_m.at[j, back], south)
        second_p[j] = a, b

    def relay_r(n):
        if n < 2:
            take(first_r[n], rin_p.at[n])
            rs_p[n] = (f(d_ref[n, every, along(1)]) + f(rin_p[n])).astype(BF)
            second_r[n] = push(rs_p.at[n], rr_p.at[n], east)
        else:
            take(first_r[n], rin_m.at[n - 2])
            rs_m[n - 2] = (f(d_ref[n, every, along(-1)]) + f(rin_m[n - 2])).astype(BF)
            second_r[n] = push(rs_m.at[n - 2], rr_m.at[n], west)

    def settle(j):
        zz = (z + j) % NZ
        a, b = plain_p[j]
        take(a, pr_p.at[j, back])
        take(b, pr_m.at[j, front])
        a, b = second_p[j]
        take(a, pr_p.at[j, front])
        take(b, pr_m.at[j, back])
        pz_s[j] = (f(d_ref[y, zz, pl.ds(0, PR)]) + f(pr_p[j]) + f(pr_m[j])).astype(BF)
        if j:
            third_p[j] = push(pz_s.at[j], pz_r.at[j], at(dz=j))

    def settle_r(n):
        take(second_r[n], (rr_p if n < 2 else rr_m).at[n])
        take(plain_r[n], (rr_m if n < 2 else rr_p).at[n])
        ry_s[n] = (f(d_ref[n, every, along(0)]) + f(rr_p[n]) + f(rr_m[n])).astype(BF)

    for j in Z_ORDER[:3]:
        plain(j)
    for n in range(NZ + 3):
        if n < NZ:
            if n < NY:
                relay_r(n)
            relay(Z_ORDER[n])
            if n + 3 < NZ:
                plain(Z_ORDER[n + 3])
        if n >= 3:
            if n < 3 + NY:
                settle_r(n - 3)
            settle(Z_ORDER[n - 3])
        if n == 2 + NY:
            third_r = {k: push(ry_s.at[(y + k) % NY], ry_r.at[k], at(dy=k)) for k in (2, 1, 3)}
        if n == 4 + NY:
            total = f(ry_s[y])
            for k in (1, 2, 3):
                take(third_r[k], ry_r.at[k])
                total = total + f(ry_r[k])
            rz_s[...] = total.astype(BF)
            fourth_r = {
                j: push(rz_s.at[(z + j) % NZ], rz_r.at[j], at(dz=j)) for j in Z_ORDER[:-1]
            }

    total = f(rz_s[z])
    for j in range(1, NZ):
        take(fourth_r[j], rz_r.at[j])
        total = total + f(rz_r[j])
    rx_s[...] = total
    fifth_r = {k: push(rx_s, rx_r.at[k], at(dx=k)) for k in (2, 1, 3)}
    total = f(pz_s[0])
    for j in range(1, NZ):
        take(third_p[j], pz_r.at[j])
        total = total + f(pz_r[j])
    px_s[...] = total
    fourth_p = {k: push(px_s, px_r.at[k], at(dx=k)) for k in (2, 1, 3)}
    held[along(0), :] = rx_s[...]
    for k in (1, 2, 3):
        take(fifth_r[k], rx_r.at[k])
        held[along(-k), :] = rx_r[k]
    counts = held[128:144]
    weights = []
    for k in range(CLS_DEV):
        weight = jnp.zeros((KF, KF), F32)
        for b in range(BINS):
            ctf = ctf_ref[b]
            weight = weight + counts[2:3, k * BINS + b : k * BINS + b + 1] * (ctf * ctf)
        weights.append(weight)
    for table in tables:
        table.wait()
    total = px_s[...]
    for k in (1, 2, 3):
        take(fourth_p[k], px_r.at[k])
        total = total + px_r[k]
    held[0:PR] = total

    sums = held[...]
    spread = pick(left_ref[...], sums)
    diag, mid = lower_masks(2 * KF)
    extra = spread[512:768]
    parts = jnp.concatenate(
        [spread[256:512], jnp.where(diag, extra, 0.0), jnp.where(mid, extra, 0.0)], 1
    )
    high = parts.astype(BF)
    rest = (parts - f(high)).astype(BF)
    data = spread[0:256] + dot(high, expand_ref[...]) + dot(rest, expand_ref[...])
    packed = pick(chooser, jnp.concatenate([data[:, :KF], data[:, KF:]] + weights, 0))
    sb[...] = packed.reshape(OWNERS, 16, KF)
    rb[cls] = sb[cls]
    used = pl.ds(0, 12)
    went = {
        k: push(sb.at[(cls + k) % OWNERS, used], rb.at[cls, used], owner_at(k)) for k in range(1, OWNERS)
    }
    place = lax.broadcasted_iota(jnp.int32, (KF, OWNERS * 16), 0)
    kind = lax.shift_right_arithmetic(
        lax.broadcasted_iota(jnp.int32, (KF, OWNERS * 16), 1) & 15, 2
    )
    hit = place == cell
    hits = jnp.concatenate(
        [jnp.where(hit & (kind == c), 1.0, 0.0).astype(BF) for c in range(3)], 0
    )
    for k in range(1, OWNERS):
        rb[(cls - k) % OWNERS, 12:16] = jnp.zeros((4, KF), F32)
    for k in range(1, OWNERS):
        take(went[k], rb.at[(cls - k) % OWNERS, used])

    volume = pick(hits, rb[...].reshape(OWNERS * 16, KF))
    scale = 1.0 / (volume[2 * KF :] + 1.0)
    w_re, w_im = volume[:KF] * scale, volume[KF : 2 * KF] * scale
    wz_s[:, 0:KF] = w_re.astype(BF)
    wz_s[:, KF : 2 * KF] = w_im.astype(BF)
    i = push(wz_s, wz_r, twin)
    bins[3 * SHELLS :, :] = jnp.zeros((SHELLS, KF), F32)

    def collect(q, v):
        for s in range(SHELLS):
            part = jnp.sum(jnp.where(shell == s, v, 0.0), axis=0, keepdims=True)
            bins[q * SHELLS + s : q * SHELLS + s + 1, :] = part

    collect(1, w_re * w_re + w_im * w_im)
    take(i, wz_r)
    o_re, o_im = f(wz_r[:, 0:KF]), f(wz_r[:, KF : 2 * KF])
    collect(0, w_re * o_re + w_im * o_im)
    collect(2, o_re * o_re + o_im * o_im)

    def across(v):
        return lax.dot_general(
            jnp.ones((8, KF), BF), v, (((1,), (1,)), ((), ())), preferred_element_type=F32
        )

    rest = bins[...]
    sums = jnp.zeros((8, 4 * SHELLS), F32)
    for _ in range(3):
        high = rest.astype(BF)
        sums = sums + across(high)
        rest = rest - f(high)
    sz_s[...] = sums
    tags = {j: push(sz_s, sz_r.at[j], at(dz=j)) for j in Z_ORDER[:-1]}
    for j, tag in tags.items():
        take(tag, sz_r.at[j])
        sums = sums + sz_r[j]
    sx_s[...] = sums
    tags = {k: push(sx_s, sx_r.at[k[0], k[1]], device) for k, device in plane_peers.items()}
    for k, tag in tags.items():
        take(tag, sx_r.at[k[0], k[1]])
        sums = sums + sx_r[k[0], k[1]]
    sums = [sums[0:1, q * SHELLS : (q + 1) * SHELLS] for q in range(3)]
    fsc = sums[0] / jnp.maximum(jnp.sqrt(sums[1] * sums[2]), 1.0)
    fsc = jnp.maximum(fsc, 0.0)
    gain = jnp.sqrt(2.0 * fsc / (1.0 + fsc))
    voxel = jnp.zeros((KF, KF), F32)
    for s in range(SHELLS):
        voxel = jnp.where(shell == s, gain[:, s : s + 1], voxel)
    o_ref[0, :, 0:KF] = w_re * voxel
    o_ref[0, :, KF : 2 * KF] = w_im * voxel
    for out in sent:
        out.wait_send()


def left_table():
    table = np.zeros((768, ROWS), np.float32)
    for k in range(CLS_DEV):
        for r in range(KF):
            if r < HK:
                table[k * KF + r, k * HK + r] = 1.0
            elif r > HK:
                table[256 + k * KF + r, k * HK + KF - r] = 1.0
            table[512 + k * KF + r, 2 * HK + k] = 1.0
    return table


def shards(images, references, image_owner, image_class, defocus_bin, slice_cells):
    cos_table, sin_table = dft_tables()
    cs = jnp.asarray(np.concatenate([cos_table, sin_table], 1))
    cst = jnp.asarray(np.concatenate([cos_table.T, sin_table.T], 0))
    both = jnp.asarray(
        np.concatenate(
            [np.concatenate([cos_table, sin_table], 1), np.concatenate([cos_table.T, sin_table.T], 0)], 0
        )
    )
    widen = jnp.asarray(
        np.concatenate(
            [
                np.concatenate([cos_table.T, sin_table.T], 1),
                np.concatenate([-sin_table.T, cos_table.T], 1),
            ],
            0,
        )
    )
    combine = jnp.asarray(np.concatenate([cos_table, -sin_table], 1))
    ctf = jnp.asarray(ctf_table())
    expand = jnp.asarray(expand_tables(), BF)
    turn = jnp.asarray(row_turn(), BF)
    left = jnp.asarray(left_table(), BF)
    local = images.shape[0]
    vmem = pl.BlockSpec(memory_space=pltpu.VMEM)
    anywhere = pl.BlockSpec(memory_space=pltpu.HBM)
    dma = pltpu.SemaphoreType.DMA

    spectra = pl.pallas_call(
        gather_kernel,
        name="gather_references",
        out_shape=jax.ShapeDtypeStruct((NY, NZ, ROWS, 2 * KF), BF),
        in_specs=[anywhere] * 2,
        out_specs=vmem,
        scratch_shapes=[
            pltpu.VMEM((CLS_DEV, PIX, PIX), BF), pltpu.VMEM((2 * PIX, 2 * KF), BF),
            pltpu.VMEM((ROWS, 2 * KF), BF), dma((2,)), dma((GATHER_SEMS,)), dma((GATHER_SEMS,)),
        ],
        compiler_params=pltpu.CompilerParams(
            collective_id=0, has_side_effects=True, vmem_limit_bytes=44 << 20
        ),
    )(references[0], both)

    partial = pl.pallas_call(
        image_kernel,
        name="image_terms",
        out_shape=jax.ShapeDtypeStruct((OWNERS, ROWS, 2 * KF), BF),
        grid_spec=pltpu.PrefetchScalarGridSpec(
            num_scalar_prefetch=3,
            grid=(local // GROUP,),
            in_specs=[
                pl.BlockSpec((GROUP, PIX, PIX), lambda i, *_: (i, 0, 0)),
                *[vmem] * 8,
            ],
            out_specs=vmem,
            scratch_shapes=[pltpu.VMEM((OWNERS, ROWS, 2 * KF), F32)],
        ),
        compiler_params=pltpu.CompilerParams(
            dimension_semantics=("arbitrary",), vmem_limit_bytes=44 << 20
        ),
    )(
        image_owner[:, 0], image_class, defocus_bin, images,
        spectra.reshape(OWNERS, ROWS, 2 * KF), ctf, cs, cst, widen, combine, expand, turn,
    )

    def buf(*shape):
        return pltpu.VMEM(shape, BF)

    wide = 2 * KF
    return pl.pallas_call(
        reduce_kernel,
        name="reduce_maps",
        out_shape=jax.ShapeDtypeStruct((1, KF, 2 * KF), F32),
        in_specs=[vmem] * 3 + [anywhere] * 2,
        out_specs=vmem,
        scratch_shapes=[
            buf(768, 256), buf(768, ROWS), buf(NZ, PA, wide), buf(NZ, PR - PA, wide),
            buf(NZ, PA, wide), buf(NZ, PR - PA, wide), buf(NZ, PR, wide), buf(NZ, PR, wide),
            buf(NZ, PR, wide), buf(NZ, PR, wide),
            pltpu.VMEM((PR, wide), F32), pltpu.VMEM((NX, PR, wide), F32),
            buf(2, NZ, 16, wide), buf(2, NZ, 16, wide), buf(2, NZ, 16, wide), buf(2, NZ, 16, wide),
            buf(NY, NZ, 16, wide), buf(NY, NZ, 16, wide),
            buf(NY, NZ, 16, wide), buf(NY, NZ, 16, wide), buf(NZ, 16, wide), buf(NZ, 16, wide),
            pltpu.VMEM((16, wide), F32), pltpu.VMEM((NX, 16, wide), F32), pltpu.VMEM((ROWS, wide), F32),
            pltpu.VMEM((OWNERS, 16, KF), F32), pltpu.VMEM((OWNERS, 16, KF), F32),
            buf(KF, wide), buf(KF, wide),
            pltpu.VMEM((8, 4 * SHELLS), F32), pltpu.VMEM((NZ, 8, 4 * SHELLS), F32),
            pltpu.VMEM((8, 4 * SHELLS), F32), pltpu.VMEM((NY, NX, 8, 4 * SHELLS), F32),
            pltpu.VMEM((4 * SHELLS, KF), F32),
            dma((2,)), dma((REDUCE_SEMS,)), dma((REDUCE_SEMS,)),
        ],
        compiler_params=pltpu.CompilerParams(
            collective_id=1, has_side_effects=True, vmem_limit_bytes=40 << 20
        ),
    )(partial.reshape(NY, NZ, ROWS, 2 * KF), ctf, slice_cells, expand, left)


def solution(mesh):
    placed = (
        P(("half", "cls", "tile"), None, None),
        P("half", "cls", None, None),
        P(("half", "cls", "tile"), None),
        P(("half", "cls", "tile")),
        P(("half", "cls", "tile")),
        P(),
    )
    return jax.shard_map(
        shards,
        mesh=mesh,
        in_specs=placed,
        out_specs=P("half", ("cls", "tile"), None),
        check_vma=False,
    )
```
